512 devices in a mesh: shot: 128 (over z, x, core), freq: 4 (over y).
Axes of the slice: x: 4, y: 4, z: 16, core: 2. Of those that a mesh axis runs over, the one named last changes fastest.
Arguments:
- traces: float32 [4, 2, 524288], P('freq', None, 'shot'), may hold values from -6 to 6
- trace_slot: int32 [524288], P('shot'), may hold values from 0 to 8191, as said below
- trace_cmp: int32 [524288], P('shot'), may hold values from 0 to 3
- trace_bin: int32 [524288], P('shot'), may hold values from 0 to 511
- prior_weight: float32 [2048, 256], P('shot'), may hold values from 0.5 to 2
Outputs:
- primaries: float32 [4, 2, 524288], P('freq', None, 'shot')
- radon_model: float32 [4, 2, 2048, 256], P('freq', None, 'shot')
The draws below stay inside these ranges and needn't reach their ends.
Inputs may be any that keep to these rules, and one draw needn't show every extreme that they name: On each index of shot the values are distinct; trace_slot // 16 is the owning shot index of the trace's CMP gather times 4 plus the quarter of that owner's gathers, so at most 16 traces of one index of shot go to one quarter of one owner; in every draw one such quarter receives exactly 16 traces from every index of shot.
All inputs are finite; a program needn't handle non-finite values.
Results may differ from the reference program's by a relative error of at most 0.0085.
Values sent between devices are 32-bit elements; how exact they have to be, the bound alone decides.
A program may use at most 64 MiB of HBM per device.

```python
import math
import jax
import jax.numpy as jnp
from jax import lax

BINS = 512
Q = 256
CG_STEPS = 8
IRLS = 2
TR_DEV = 4096
FREQS = 4
CMPS = 2048
CMP_Q = 4
CAPQ = 16
TRACES = 524288
N_SHOT = 128
N_FREQ = 4


def draw_trace_slot(key, part):
    slot_total = N_SHOT * N_FREQ * CAPQ
    group_total = N_SHOT * N_FREQ
    full_group = jax.random.randint(jax.random.fold_in(key, 11), (), 0, group_total)
    favour = jax.random.randint(jax.random.fold_in(key, 12), (group_total,), 0, 4)
    slot_group = jnp.arange(slot_total, dtype=jnp.int32) // CAPQ
    base_score = -favour[slot_group] * 65536
    base_score = jnp.where(slot_group == full_group, -(1 << 22), base_score)

    def one_device(device):
        device_key = jax.random.fold_in(jax.random.fold_in(key, 13), device)
        jitter = jax.random.randint(device_key, (slot_total,), 0, 1 << 18)
        ranking = jnp.argsort(base_score + jitter, stable=True)
        chosen = ranking[:TR_DEV].astype(jnp.int32)
        return jax.random.permutation(jax.random.fold_in(device_key, 5), chosen)
    return jax.vmap(one_device)(jnp.arange(N_SHOT, dtype=jnp.int32)).reshape(-1).astype(jnp.int32)


def touch_ends(values, stream_key, smallest, top_value):
    shape = values.shape
    place = [jax.random.randint(jax.random.fold_in(stream_key, axis), (), 0, shape[axis]) for axis in range(len(shape))]
    values = values.at[tuple(place)].set(smallest)
    longest = shape.index(max(shape))
    place[longest] = (place[longest] + 1) % shape[longest]
    return values.at[tuple(place)].set(top_value)


def steps_of(key, extent, split, least, largest):
    def one(dim, shards_of):
        heights = jax.random.uniform(jax.random.fold_in(jax.random.fold_in(key, 6), dim), (shards_of,), jnp.float32, least / len(split), largest / len(split))
        return jnp.repeat(jnp.exp(heights), extent[dim] // shards_of).reshape((-1,) + (1,) * (len(extent) - dim - 1))

    factor_of = one(*split[0])
    for cut in split[1:]:
        factor_of = factor_of * one(*cut)
    return factor_of


def noise(own_key, dims, scale, bound, shards=(), kind=jnp.bfloat16):
    result = scale * jax.random.normal(own_key, dims, jnp.float32)
    if shards:
        result = result * steps_of(own_key, dims, shards, -0.22, 0.18)
    return jnp.clip(result, -bound, bound).astype(kind)


def setup_inputs(seed: int = 0) -> dict:
    streams_of = jax.random.split(jax.random.key(seed), 6)
    return {
        "traces": noise(streams_of[0], (FREQS, 2, TRACES), 1.0, 6.0, ((0, 4), (2, 128)), jnp.float32),
        "trace_slot": draw_trace_slot(jax.random.fold_in(streams_of[5], 71), 0),
        "trace_cmp": touch_ends(jax.random.randint(streams_of[2], (TRACES,), 0, CMP_Q), jax.random.fold_in(streams_of[2], 1), 0, CMP_Q - 1).astype(jnp.int32),
        "trace_bin": touch_ends(jax.random.randint(streams_of[3], (TRACES,), 0, BINS), jax.random.fold_in(streams_of[3], 1), 0, BINS - 1).astype(jnp.int32),
        "prior_weight": jnp.clip(jnp.exp(math.log(2.0) - 1.3862944 * jax.random.uniform(streams_of[4], (CMPS, Q), jnp.float32) ** steps_of(streams_of[4], (CMPS, Q), ((0, 128),), -0.2, 0.2)), 0.5, 2.0),
    }


MU_SCALE = 0.5
ENERGY_FLOOR = 0.5
SMALL_EPS = 1e-6


def radon_table(freq_ids, freq_total):
    nu_value = 0.5 + 0.5 * freq_ids.astype(jnp.float32) / freq_total
    curvature = jnp.arange(Q).astype(jnp.float32) - (Q // 8)
    offset = (jnp.arange(BINS).astype(jnp.float32) + 0.5) / BINS
    phase = (2.0 * math.pi) * nu_value[:, None, None] * curvature[None, :, None] * (offset * offset)[None, None, :]
    return jnp.cos(phase), -jnp.sin(phase)


def spread(operand, table_part):
    return jnp.einsum('fcq,fqb->fcb', operand, table_part, precision=lax.Precision.HIGHEST)


def collect(operand, table_part):
    return jnp.einsum('fcb,fqb->fcq', operand, table_part, precision=lax.Precision.HIGHEST)


def forward(field, cos_table, sin_table):
    real_part = spread(field[:, 0], cos_table) - spread(field[:, 1], sin_table)
    imag_part = spread(field[:, 1], cos_table) + spread(field[:, 0], sin_table)
    return jnp.stack([real_part, imag_part], axis=1)


def adjoint(binned, cos_table, sin_table):
    real_part = collect(binned[:, 0], cos_table) + collect(binned[:, 1], sin_table)
    imag_part = collect(binned[:, 1], cos_table) - collect(binned[:, 0], sin_table)
    return jnp.stack([real_part, imag_part], axis=1)


def inner_sum(first, second):
    return jnp.sum(first * second, axis=(1, 3))[:, None, :, None]


def conjugate(right_side, counts, weight, cos_table, sin_table):
    damping = MU_SCALE * BINS * weight[None, None]
    fold_map = counts[None, None]
    solution = jnp.zeros_like(right_side)
    residual = right_side
    direction = right_side
    norm_now = inner_sum(residual, residual)
    for cg_step in range(CG_STEPS):
        image_vec = adjoint(fold_map * forward(direction, cos_table, sin_table), cos_table, sin_table) + damping * direction
        step_size = norm_now / inner_sum(direction, image_vec)
        solution = solution + step_size * direction
        residual = residual - step_size * image_vec
        norm_next = inner_sum(residual, residual)
        direction = residual + (norm_next / norm_now) * direction
        norm_now = norm_next
    return solution


def reweigh(energy):
    average = jnp.mean(energy, axis=1, keepdims=True)
    return (average + SMALL_EPS) / (energy + ENERGY_FLOOR * average + SMALL_EPS)


def reference(traces, trace_slot, trace_cmp, trace_bin, prior_weight):
    cell_index = ((trace_slot // CAPQ) * CMP_Q + trace_cmp) * BINS + trace_bin
    flat = traces.reshape(FREQS * 2, TRACES).T
    binned = jax.ops.segment_sum(flat, cell_index, num_segments=CMPS * BINS).T.reshape(FREQS, 2, CMPS, BINS)
    counts = jax.ops.segment_sum(jnp.ones((TRACES,), jnp.float32), cell_index, num_segments=CMPS * BINS).reshape(CMPS, BINS)
    cos_table, sin_table = radon_table(jnp.arange(FREQS, dtype=jnp.int32), FREQS)
    right_side = adjoint(binned, cos_table, sin_table)
    weight = prior_weight
    radon_model = right_side
    for irls_pass in range(IRLS):
        if irls_pass > 0:
            weight = reweigh(jnp.sum(radon_model * radon_model, axis=(0, 1)))
        radon_model = conjugate(right_side, counts, weight, cos_table, sin_table)
    multiple_mask = (jnp.arange(Q) >= Q // 4).astype(jnp.float32)
    predicted = forward(radon_model * multiple_mask, cos_table, sin_table).reshape(FREQS, 2, CMPS * BINS)
    primaries = traces - predicted[:, :, cell_index]
    return primaries, radon_model
```

```python
import math

import jax
import jax.numpy as jnp
from jax import lax
from jax.experimental import pallas as pl
from jax.experimental.pallas import tpu as pltpu
from jax.sharding import PartitionSpec as P

BINS = 512
Q = 256
HALF = 128
CG_STEPS = 8
KEPT = 3
MU_SCALE = 0.5
ENERGY_FLOOR = 0.5
SMALL_EPS = 1e-06

NZ = 16
NU = 8
NF = 4
CMP = 16
TRACES = 4096
GROUP = 1024
MESH = pl.DeviceIdType.MESH
F32 = jnp.float32
BF16 = jnp.bfloat16

NN = (((1,), (0,)), ((), ()))
NT = (((1,), (1,)), ((), ()))


def mxu(a, b, dims=NN):
    return lax.dot_general(a, b, dims, preferred_element_type=F32)


def split(v, pieces=2):
    out = [v.astype(BF16)]
    for _ in range(pieces - 1):
        v = v - out[-1].astype(F32)
        out.append(v.astype(BF16))
    return out


def reverse_lanes(v, flip):
    n = v.shape[0]
    out = mxu(jnp.concatenate(split(v, 3), axis=0), flip)
    return out[:n] + out[n : 2 * n] + out[2 * n :]


def sincos(k):
    quadrant = (k + (1 << 21)) >> 22
    rem = (k - (quadrant << 22)).astype(F32)
    t = rem * (2.0 * math.pi / (1 << 24))
    u = t * t
    s = t + t * u * (-1.0 / 6 + u * (1.0 / 120 + u * (-1.0 / 5040 + u * (1.0 / 362880))))
    c = 1.0 + u * (-0.5 + u * (1.0 / 24 + u * (-1.0 / 720 + u * (1.0 / 40320 + u * (-1.0 / 3628800)))))
    quadrant = quadrant & 3
    odd = (quadrant & 1) == 1
    cos = jnp.where(odd, s, c)
    sin = jnp.where(odd, c, s)
    cos = jnp.where((quadrant == 1) | (quadrant == 2), -cos, cos)
    sin = jnp.where(quadrant >= 2, -sin, sin)
    return cos, sin


def kernel(
    traces_hbm, slot_hbm, cmp_hbm, bin_hbm, weight_hbm, primaries, radon_model,
    traces, slot_in, cmp_in, bin_in, weight_in, in_sems,
    dest_hot, trace_hot, slot_low, slot_hot, row_h, row_s,
    table, table_low, table_t, table_t_low, counts_ref,
    send_a, recv_a, pair_code, recv_v, recv_c, energy_own, energy_all, send_r, recv_r, recv_t,
    a_send, a_recv, b_send, b_recv, c_send, c_recv, e_send, e_recv, r_send, r_recv, t_send, t_recv,
):
    inputs = [
        pltpu.make_async_copy(source, target, in_sems.at[i])
        for i, (source, target) in enumerate(
            (
                (slot_hbm, slot_in),
                (traces_hbm, traces),
                (bin_hbm, bin_in),
                (cmp_hbm, cmp_in),
                (weight_hbm, weight_in),
            )
        )
    ]
    for copy in inputs:
        copy.start()

    shot = lax.axis_index("shot")
    f = lax.axis_index("freq")
    z = shot // NU
    x_core = lax.rem(shot, NU)
    core = lax.rem(x_core, 2)
    u = core * 4 + x_core // 2

    def shot_of(z_at, u_at):
        return z_at * NU + lax.rem(u_at, 4) * 2 + u_at // 4

    barrier = pltpu.get_barrier_semaphore()
    for k in range(1, NU):
        peer = shot_of(z, lax.rem(u + k, NU))
        pl.semaphore_signal(barrier, inc=1, device_id={"shot": peer}, device_id_type=MESH)
    for k in range(1, NZ):
        peer = shot_of(lax.rem(z + k, NZ), u)
        pl.semaphore_signal(barrier, inc=1, device_id={"shot": peer}, device_id_type=MESH)
    for k in range(1, NF):
        pl.semaphore_signal(barrier, inc=1, device_id={"freq": lax.rem(f + k, NF)}, device_id_type=MESH)

    lane = lax.broadcasted_iota(jnp.int32, (8, 128), 1)
    sub64 = lax.broadcasted_iota(jnp.int32, (64, 128), 0)
    sub128 = lax.broadcasted_iota(jnp.int32, (128, 128), 0)

    for copy in inputs:
        copy.wait()

    @pl.loop(0, TRACES // GROUP)
    def _(step):
        rows = pl.ds(pl.multiple_of(step * 8, 8), 8)
        slot, bins = slot_in[rows, :], bin_in[rows, :]
        dest = (((slot >> 6) & 1) * 4 + ((slot >> 7) & 3)) * NZ + (slot >> 9)
        within = slot & 63
        row_s[rows, :] = within
        high = (bins >> 7) * 16 + ((slot >> 4) & 3) * 4 + cmp_in[rows, :] + 1
        low = bins & 127
        high, low = high.astype(F32), low.astype(F32)
        for i in range(8):
            lanes = pl.ds(pl.multiple_of(step * GROUP + i * 128, 128), 128)
            re_h, re_l = split(traces[0, 0:1, lanes])
            im_h, im_l = split(traces[0, 1:2, lanes])
            dest_hot[:, lanes] = jnp.where(sub128 == dest[i : i + 1], 1.0, 0.0).astype(BF16)
            mask = sub64 == within[i : i + 1]
            for j, piece in enumerate((re_h, im_h, re_l, im_l, high[i : i + 1], low[i : i + 1])):
                trace_hot[64 * j : 64 * (j + 1), lanes] = jnp.where(mask, piece.astype(F32), 0.0).astype(BF16)

    placed = mxu(dest_hot[...], trace_hot[...], NT)
    values = placed[:, 0:128] + placed[:, 128:256]
    codes = placed[:, 256:384]
    turned = pltpu.roll(codes, 64, 1)
    lane_full = lax.broadcasted_iota(jnp.int32, (128, 128), 1)
    codes = jnp.where(lane_full < 64, 128.0 * codes + turned, 128.0 * turned + codes)
    codes = jnp.where(lane_full // 64 == core, codes, 0.0)
    send_a[:, 0] = values.reshape(NU, NZ, 128)
    send_a[:, 1] = codes.reshape(NU, NZ, 128)

    pl.semaphore_wait(barrier, NU + NZ + NF - 3)

    def copy_a(k):
        peer = lax.rem(u + k, NU)
        return pltpu.make_async_remote_copy(
            send_a.at[peer], recv_a.at[u], a_send.at[k], a_recv.at[k],
            device_id={"shot": shot_of(z, peer)}, device_id_type=MESH,
        )

    for k in range(1, NU):
        copy_a(k).start()
    recv_a[u] = send_a[u]

    factor = math.sqrt(2.0)
    odd_m = 2 * lax.broadcasted_iota(jnp.int32, (64, HALF), 1) + 1

    @pl.loop(0, BINS // 64)
    def _(step):
        b = 2 * (lax.broadcasted_iota(jnp.int32, (64, HALF), 0) + step * 64) + 1
        cos, sin = sincos((4 + f) * odd_m * b * b)
        high, low = split(factor * cos)
        rows = pl.ds(pl.multiple_of(step * 64, 64), 64)
        table[rows, 0:HALF] = high
        table_low[rows, 0:HALF] = low
        high, low = split(factor * sin)
        table[rows, HALF:Q] = high
        table_low[rows, HALF:Q] = low

    for k in range(1, NU):
        copy_a(k).wait_recv()
    for i in range(4):
        pair_code[i] = recv_a[i, 1] + recv_a[i + 4, 1]

    def copies_b(k):
        there = lax.rem(z + k, NZ)
        peer = {"shot": shot_of(there, u)}
        return (
            pltpu.make_async_remote_copy(
                recv_a.at[:, 0, there], recv_v.at[z], b_send.at[k], b_recv.at[k],
                device_id=peer, device_id_type=MESH,
            ),
            pltpu.make_async_remote_copy(
                pair_code.at[:, there], recv_c.at[z], c_send.at[k], c_recv.at[k],
                device_id=peer, device_id_type=MESH,
            ),
        )

    for k in (8, 7, 9, 6, 10, 5, 11, 4, 12, 3, 13, 2, 14, 1, 15):
        for copy in copies_b(k):
            copy.start()
    recv_v[z] = recv_a[:, 0, z]
    recv_c[z] = pair_code[:, z]

    odd_row = 2 * lax.broadcasted_iota(jnp.int32, (64, 128), 0) + 1

    @pl.loop(0, BINS // 128)
    def _(step):
        b = 2 * (lax.broadcasted_iota(jnp.int32, (64, 128), 1) + step * 128) + 1
        lanes = pl.ds(pl.multiple_of(step * 128, 128), 128)
        for part in range(2):
            rows = slice(part * 64, part * 64 + 64)
            cos, sin = sincos((4 + f) * (odd_row + part * 128) * b * b)
            high, low = split(factor * cos)
            table_t[rows, lanes] = high
            table_t_low[rows, lanes] = low
            rows = slice(HALF + part * 64, HALF + part * 64 + 64)
            high, low = split(factor * sin)
            table_t[rows, lanes] = high
            table_t_low[rows, lanes] = low

    b = 2 * lax.broadcasted_iota(jnp.int32, (1, BINS), 1) + 1
    shift_cos, shift_sin = sincos((4 + f) * (191 * b * b))
    flip = jnp.where(sub128 + lane_full == 127, 1.0, 0.0).astype(BF16)
    weight = weight_in[...]
    w_plus, w_minus = weight[:, HALF:], reverse_lanes(weight[:, :HALF], flip)

    lane4 = lax.broadcasted_iota(jnp.int32, (4, 128), 1)

    def bin_step(step, below, above, total):
        rows = pl.ds(pl.multiple_of(step * 8, 8), 8)
        re, im, code = [], [], []
        for at in (below, above):
            first, second = recv_v[at, 0:4], recv_v[at, 4:8]
            re.append(jnp.where(lane4 < 64, first, pltpu.roll(second, 64, 1)))
            im.append(jnp.where(lane4 < 64, pltpu.roll(first, 64, 1), second))
            code.append(recv_c[at])
        re, im = jnp.concatenate(re, axis=0), jnp.concatenate(im, axis=0)
        code = jnp.concatenate(code, axis=0).astype(jnp.int32)
        h, low = (code >> 7) - 1, code & 127
        row_h[rows, :] = h
        pieces = [p.astype(F32) for v in (re, im) for p in split(v)]
        for i in range(8):
            lanes = pl.ds(pl.multiple_of(step * GROUP + i * 128, 128), 128)
            here = slice(i * 128, i * 128 + 128)
            slot_low[:, lanes] = jnp.where(sub128 == low[i : i + 1], 1.0, 0.0).astype(BF16)
            mask = sub64 == h[i : i + 1]
            for j, piece in enumerate(pieces):
                slot_hot[64 * j : 64 * (j + 1), here] = jnp.where(mask, piece[i : i + 1], 0.0).astype(BF16)
            slot_hot[256:320, here] = jnp.where(mask, 1.0, 0.0).astype(BF16)
        lanes = pl.ds(pl.multiple_of(step * GROUP, 128), GROUP)
        return total + mxu(slot_hot[...], slot_low[:, lanes], NT)

    def bin_pair(step, total):
        for k in (step + 1, NZ - 1 - step):
            for copy in copies_b(k):
                copy.wait_recv()
        return bin_step(step, lax.rem(z + NZ - 1 - step, NZ), lax.rem(z + step + 1, NZ), total)

    binned = lax.fori_loop(0, 7, bin_pair, jnp.zeros((320, 128), F32))
    for copy in copies_b(8):
        copy.wait_recv()
    binned = bin_step(7, z, lax.rem(z + 8, NZ), binned)

    def by_bin(rows):
        return jnp.concatenate([rows[16 * i : 16 * i + 16] for i in range(4)], axis=1)

    g_re = by_bin(binned[0:64] + binned[64:128])
    g_im = by_bin(binned[128:192] + binned[192:256])
    counts_ref[...] = by_bin(binned[256:320])

    def product(v, high, low):
        n = v.shape[0]
        v_high, v_low = split(v)
        main = mxu(jnp.concatenate([v_high, v_low], axis=0), high)
        return main[:n] + (main[n:] + mxu(v_high, low))

    def forward(v):
        return product(v, table_t[...], table_t_low[...])

    def adjoint(g):
        return product(g, table[...], table_low[...])

    right_side = adjoint(
        jnp.concatenate([shift_cos * g_re - shift_sin * g_im, shift_cos * g_im + shift_sin * g_re], axis=0)
    )

    def inner(a, b):
        p = a * b
        return jnp.sum(p[:CMP] + p[CMP:], axis=1, keepdims=True)

    def both_parts(v):
        return jnp.concatenate([v, v], axis=0)

    def undamped(v):
        return adjoint(forward(v) * both_parts(counts_ref[...]))

    first_image = undamped(right_side)

    def solve(w_plus, w_minus):
        scale = 0.5 * MU_SCALE * BINS
        even, odd = scale * (w_plus + w_minus), scale * (w_plus - w_minus)

        def damp(v):
            s_re, s_im, t_re, t_im = v[:CMP, :HALF], v[CMP:, :HALF], v[:CMP, HALF:], v[CMP:, HALF:]
            return jnp.concatenate(
                [
                    jnp.concatenate([even * s_re - odd * t_im, even * t_re + odd * s_im], axis=1),
                    jnp.concatenate([even * s_im + odd * t_re, even * t_im - odd * s_re], axis=1),
                ],
                axis=0,
            )

        def image_of(direction):
            return undamped(direction) + damp(direction)

        def project(image, past, scales):
            out = image
            for old, scale in zip(past, scales):
                swapped = swap(old)
                along = both_parts(inner(old, image) * scale)
                across = both_parts(inner(swapped, image) * scale)
                out = out - (along * old + across * swapped)
            return out

        def swap(v):
            return jnp.concatenate([-v[CMP:], v[:CMP]], axis=0)

        def cg_step(state, past, scales, own):
            answer, residual, direction, norm_now = state
            image = first_image + damp(direction) if own and not past else image_of(direction)
            step_size = both_parts(norm_now / inner(direction, image))
            kept = project(image, past, scales)
            if own:
                swapped = swap(residual)
                kept = kept - both_parts(inner(swapped, image) / norm_now) * swapped
            answer = answer + step_size * direction
            residual = residual - step_size * kept
            norm_next = inner(residual, residual)
            direction = residual + both_parts(norm_next / norm_now) * direction
            return answer, residual, direction, norm_next

        state = (jnp.zeros_like(right_side), right_side, right_side, inner(right_side, right_side))
        past, scales = [], []
        for _ in range(KEPT):
            residual, norm = state[1], state[3]
            state = cg_step(state, past, scales, True)
            past.append(residual)
            scales.append(1.0 / norm)
        state = lax.fori_loop(
            KEPT, CG_STEPS - 1, lambda _, state: cg_step(state, past, scales, False), state
        )
        answer, _, direction, norm_now = state
        return answer + both_parts(norm_now / inner(direction, image_of(direction))) * direction

    def to_curvatures(v):
        root = math.sqrt(0.5)
        s_re, s_im, t_re, t_im = v[:CMP, :HALF], v[CMP:, :HALF], v[:CMP, HALF:], v[CMP:, HALF:]
        plus = root * (s_re - t_im), root * (s_im + t_re)
        minus = root * (s_re + t_im), root * (s_im - t_re)
        return plus, minus

    answer = solve(w_plus, w_minus)
    plus, minus = to_curvatures(answer)
    energy_own[:, :HALF] = plus[0] * plus[0] + plus[1] * plus[1]
    energy_own[:, HALF:] = minus[0] * minus[0] + minus[1] * minus[1]

    def copy_e(k):
        peer = lax.rem(f + k, NF)
        return pltpu.make_async_remote_copy(
            energy_own, energy_all.at[f], e_send.at[k], e_recv.at[k],
            device_id={"freq": peer}, device_id_type=MESH,
        )

    for k in (2, 1, 3):
        copy_e(k).start()
    energy_all[f] = energy_own[...]
    for k in (1, 3, 2):
        copy_e(k).wait_recv()
    energy = (energy_all[0] + energy_all[1]) + (energy_all[2] + energy_all[3])
    average = jnp.sum(energy, axis=1, keepdims=True) * (1.0 / Q)
    weight = (average + SMALL_EPS) / (energy + ENERGY_FLOOR * average + SMALL_EPS)
    answer = solve(weight[:, :HALF], weight[:, HALF:])
    plus, minus = to_curvatures(answer)

    root = math.sqrt(0.5)
    keep = lax.broadcasted_iota(jnp.int32, (CMP, HALF), 1) < 64
    low_re, low_im = jnp.where(keep, minus[0], 0.0), jnp.where(keep, minus[1], 0.0)
    masked = jnp.concatenate(
        [
            jnp.concatenate([root * (plus[0] + low_re), root * (plus[1] - low_im)], axis=1),
            jnp.concatenate([root * (plus[1] + low_im), root * (low_re - plus[0])], axis=1),
        ],
        axis=0,
    )
    field = forward(masked)
    p_re = shift_cos * field[:CMP] + shift_sin * field[CMP:]
    p_im = shift_cos * field[CMP:] - shift_sin * field[:CMP]
    predicted = jnp.concatenate(
        [p[:, 128 * i : 128 * i + 128] for p in (p_re, p_im) for i in range(4)], axis=0
    )
    predicted = jnp.concatenate(split(predicted), axis=1)

    def copy_r(k):
        there = lax.rem(z + k, NZ)
        return pltpu.make_async_remote_copy(
            send_r.at[there], recv_r.at[z], r_send.at[k], r_recv.at[k],
            device_id={"shot": shot_of(there, u)}, device_id_type=MESH,
        )

    lane8 = lax.broadcasted_iota(jnp.int32, (8, 128), 1)

    def predict(step, below, above):
        rows = pl.ds(pl.multiple_of(step * 8, 8), 8)
        low = slot_low[:, pl.ds(pl.multiple_of(step * GROUP, 128), GROUP)]
        found = mxu(predicted, jnp.concatenate([low, low], axis=0))
        h = row_h[rows, :]
        got_re, got_im = [], []
        for i in range(8):
            mask = sub64 == h[i : i + 1]
            here = slice(i * 128, i * 128 + 128)
            got_re.append(jnp.sum(jnp.where(mask, found[:64, here], 0.0), axis=0, keepdims=True))
            got_im.append(jnp.sum(jnp.where(mask, found[64:, here], 0.0), axis=0, keepdims=True))
        got_re, got_im = jnp.concatenate(got_re, axis=0), jnp.concatenate(got_im, axis=0)
        first = jnp.where(lane8 < 64, got_re, pltpu.roll(got_im, 64, 1))
        second = jnp.where(lane8 < 64, pltpu.roll(got_re, 64, 1), got_im)
        for i, at in enumerate((below, above)):
            send_r[at, 0:4] = first[4 * i : 4 * i + 4]
            send_r[at, 4:8] = second[4 * i : 4 * i + 4]

    predict(7, z, lax.rem(z + 8, NZ))
    copy_r(8).start()
    recv_r[z] = send_r[z]

    @pl.loop(0, 7)
    def _(back):
        step = 6 - back
        predict(step, lax.rem(z + NZ - 1 - step, NZ), lax.rem(z + step + 1, NZ))
        copy_r(NZ - 1 - step).start()
        copy_r(step + 1).start()

    for part in range(2):
        radon_model[0, part, :, 0:HALF] = reverse_lanes(minus[part], flip)
        radon_model[0, part, :, HALF:Q] = plus[part]

    for k in range(1, NZ):
        copy_r(k).wait_recv()

    def copy_t(k):
        peer = lax.rem(u + k, NU)
        return pltpu.make_async_remote_copy(
            recv_r.at[:, peer], recv_t.at[u], t_send.at[k], t_recv.at[k],
            device_id={"shot": shot_of(z, peer)}, device_id_type=MESH,
        )

    for k in range(1, NU):
        copy_t(k).start()
    recv_t[u] = recv_r[:, u]
    for k in range(1, NU):
        copy_t(k).wait_recv()

    by_slot = jnp.concatenate(split(recv_t[...].reshape(128, 128).T), axis=1)

    @pl.loop(0, TRACES // GROUP)
    def _(step):
        rows = pl.ds(pl.multiple_of(step * 8, 8), 8)
        hot = dest_hot[:, pl.ds(pl.multiple_of(step * GROUP, 128), GROUP)]
        found = mxu(by_slot, jnp.concatenate([hot, hot], axis=0))
        within = row_s[rows, :]
        for i in range(8):
            mask = sub64 == within[i : i + 1]
            here = slice(i * 128, i * 128 + 128)
            lanes = pl.ds(pl.multiple_of(step * GROUP + i * 128, 128), 128)
            got = jnp.sum(jnp.where(mask, found[:64, here], 0.0), axis=0, keepdims=True)
            primaries[0, 0:1, lanes] = traces[0, 0:1, lanes] - got
            got = jnp.sum(jnp.where(mask, found[64:, here], 0.0), axis=0, keepdims=True)
            primaries[0, 1:2, lanes] = traces[0, 1:2, lanes] - got

    for k in range(1, NU):
        copy_a(k).wait_send()
        copy_t(k).wait_send()
    for k in range(1, NZ):
        for copy in copies_b(k):
            copy.wait_send()
        copy_r(k).wait_send()
    for k in range(1, NF):
        copy_e(k).wait_send()


def per_device(traces, trace_slot, trace_cmp, trace_bin, prior_weight):
    rows = TRACES // 128
    vmem = pl.BlockSpec(memory_space=pltpu.VMEM)
    dma = pltpu.SemaphoreType.DMA
    return pl.pallas_call(
        kernel,
        out_shape=(
            jax.ShapeDtypeStruct((1, 2, TRACES), F32),
            jax.ShapeDtypeStruct((1, 2, CMP, Q), F32),
        ),
        in_specs=[pl.BlockSpec(memory_space=pltpu.HBM)] * 5,
        out_specs=(vmem, vmem),
        scratch_shapes=[
            pltpu.VMEM((1, 2, TRACES), F32),
            pltpu.VMEM((rows, 128), jnp.int32),
            pltpu.VMEM((rows, 128), jnp.int32),
            pltpu.VMEM((rows, 128), jnp.int32),
            pltpu.VMEM((CMP, Q), F32),
            dma((5,)),
            pltpu.VMEM((128, TRACES), BF16),
            pltpu.VMEM((384, TRACES), BF16),
            pltpu.VMEM((128, 8192), BF16),
            pltpu.VMEM((320, GROUP), BF16),
            pltpu.VMEM((64, 128), jnp.int32),
            pltpu.VMEM((rows, 128), jnp.int32),
            pltpu.VMEM((BINS, Q), BF16),
            pltpu.VMEM((BINS, Q), BF16),
            pltpu.VMEM((Q, BINS), BF16),
            pltpu.VMEM((Q, BINS), BF16),
            pltpu.VMEM((CMP, BINS), F32),
            pltpu.VMEM((NU, 2, NZ, 128), F32),
            pltpu.VMEM((NU, 2, NZ, 128), F32),
            pltpu.VMEM((4, NZ, 128), F32),
            pltpu.VMEM((NZ, 8, 128), F32),
            pltpu.VMEM((NZ, 4, 128), F32),
            pltpu.VMEM((CMP, Q), F32),
            pltpu.VMEM((NF, CMP, Q), F32),
            pltpu.VMEM((NZ, NU, 128), F32),
            pltpu.VMEM((NZ, NU, 128), F32),
            pltpu.VMEM((NU, NZ, 128), F32),
            dma((NU,)), dma((NU,)), dma((NZ,)), dma((NZ,)), dma((NZ,)), dma((NZ,)),
            dma((NF,)), dma((NF,)), dma((NZ,)), dma((NZ,)), dma((NU,)), dma((NU,)),
        ],
        compiler_params=pltpu.CompilerParams(
            collective_id=0, has_side_effects=True, vmem_limit_bytes=32 * 1024 * 1024
        ),
        name="radon",
    )(
        traces,
        trace_slot.reshape(rows, 128),
        trace_cmp.reshape(rows, 128),
        trace_bin.reshape(rows, 128),
        prior_weight,
    )


def solution(mesh):
    return jax.shard_map(
        per_device,
        mesh=mesh,
        in_specs=(P("freq", None, "shot"), P("shot"), P("shot"), P("shot"), P("shot", None)),
        out_specs=(P("freq", None, "shot"), P("freq", None, "shot", None)),
        check_vma=False,
    )
```

```python
import math

import jax
import jax.numpy as jnp
from jax import lax
from jax.experimental import pallas as pl
from jax.experimental.pallas import tpu as pltpu
from jax.sharding import PartitionSpec as P

BINS = 512
Q = 256
HALF = 128
CG_STEPS = 8
KEPT = 3
MU_SCALE = 0.5
ENERGY_FLOOR = 0.5
SMALL_EPS = 1e-06

NZ = 16
NU = 8
NF = 4
CMP = 16
TRACES = 4096
GROUP = 1024
MESH = pl.DeviceIdType.MESH
F32 = jnp.float32
BF16 = jnp.bfloat16

NN = (((1,), (0,)), ((), ()))
NT = (((1,), (1,)), ((), ()))


def mxu(a, b, dims=NN):
    return lax.dot_general(a, b, dims, preferred_element_type=F32)


def split(v, pieces=2):
    out = [v.astype(BF16)]
    for _ in range(pieces - 1):
        v = v - out[-1].astype(F32)
        out.append(v.astype(BF16))
    return out


def reverse_lanes(v, flip):
    n = v.shape[0]
    out = mxu(jnp.concatenate(split(v, 3), axis=0), flip)
    return out[:n] + out[n : 2 * n] + out[2 * n :]


def sincos(k):
    quadrant = (k + (1 << 21)) >> 22
    rem = (k - (quadrant << 22)).astype(F32)
    t = rem * (2.0 * math.pi / (1 << 24))
    u = t * t
    s = t + t * u * (-1.0 / 6 + u * (1.0 / 120 + u * (-1.0 / 5040 + u * (1.0 / 362880))))
    c = 1.0 + u * (-0.5 + u * (1.0 / 24 + u * (-1.0 / 720 + u * (1.0 / 40320 + u * (-1.0 / 3628800)))))
    quadrant = quadrant & 3
    odd = (quadrant & 1) == 1
    cos = jnp.where(odd, s, c)
    sin = jnp.where(odd, c, s)
    cos = jnp.where((quadrant == 1) | (quadrant == 2), -cos, cos)
    sin = jnp.where(quadrant >= 2, -sin, sin)
    return cos, sin


def kernel(
    traces_hbm, slot_hbm, cmp_hbm, bin_hbm, weight_hbm, primaries_hbm, radon_hbm,
    traces, slot_in, cmp_in, bin_in, weight_in, in_sems, primaries, radon_model, out_sems,
    dest_hot, trace_hot, slot_low, slot_hot, row_h, row_s,
    table, table_low, table_t, table_t_low, counts_ref,
    send_a, recv_a, send_b, recv_b, energy_own, energy_all, send_r, recv_r, recv_t,
    a_send, a_recv, b_send, b_recv, e_send, e_recv, r_send, r_recv, t_send, t_recv,
):
    inputs = [
        pltpu.make_async_copy(source, target, in_sems.at[i])
        for i, (source, target) in enumerate(
            (
                (slot_hbm, slot_in),
                (traces_hbm, traces),
                (bin_hbm, bin_in),
                (cmp_hbm, cmp_in),
                (weight_hbm, weight_in),
            )
        )
    ]
    for copy in inputs:
        copy.start()

    shot = lax.axis_index("shot")
    f = lax.axis_index("freq")
    z = shot // NU
    x_core = lax.rem(shot, NU)
    core = lax.rem(x_core, 2)
    u = core * 4 + x_core // 2

    def shot_of(z_at, u_at):
        return z_at * NU + lax.rem(u_at, 4) * 2 + u_at // 4

    barrier = pltpu.get_barrier_semaphore()
    for k in range(1, NU):
        peer = shot_of(z, lax.rem(u + k, NU))
        pl.semaphore_signal(barrier, inc=1, device_id={"shot": peer}, device_id_type=MESH)
    for k in range(1, NZ):
        peer = shot_of(lax.rem(z + k, NZ), u)
        pl.semaphore_signal(barrier, inc=1, device_id={"shot": peer}, device_id_type=MESH)
    for k in range(1, NF):
        pl.semaphore_signal(barrier, inc=1, device_id={"freq": lax.rem(f + k, NF)}, device_id_type=MESH)

    lane = lax.broadcasted_iota(jnp.int32, (8, 128), 1)
    sub64 = lax.broadcasted_iota(jnp.int32, (64, 128), 0)
    sub128 = lax.broadcasted_iota(jnp.int32, (128, 128), 0)

    for copy in inputs:
        copy.wait()

    @pl.loop(0, TRACES // GROUP)
    def _(step):
        rows = pl.ds(pl.multiple_of(step * 8, 8), 8)
        slot, bins = slot_in[rows, :], bin_in[rows, :]
        dest = (((slot >> 6) & 1) * 4 + ((slot >> 7) & 3)) * NZ + (slot >> 9)
        within = (slot + 16 * lax.rem(u, 4)) & 63
        row_s[rows, :] = within
        high = (bins >> 7) * 4 + cmp_in[rows, :] + 1
        low = bins & 127
        high, low = high.astype(F32), low.astype(F32)
        for i in range(8):
            lanes = pl.ds(pl.multiple_of(step * GROUP + i * 128, 128), 128)
            re_h, re_l = split(traces[0, 0:1, lanes])
            im_h, im_l = split(traces[0, 1:2, lanes])
            dest_hot[:, lanes] = jnp.where(sub128 == dest[i : i + 1], 1.0, 0.0).astype(BF16)
            mask = sub64 == within[i : i + 1]
            for j, piece in enumerate((re_h, im_h, re_l, im_l, high[i : i + 1], low[i : i + 1])):
                trace_hot[64 * j : 64 * (j + 1), lanes] = jnp.where(mask, piece.astype(F32), 0.0).astype(BF16)

    placed = mxu(dest_hot[...], trace_hot[...], NT)
    values = placed[:, 0:128] + placed[:, 128:256]
    codes = placed[:, 256:384]
    turned = pltpu.roll(codes, 64, 1)
    lane_full = lax.broadcasted_iota(jnp.int32, (128, 128), 1)
    codes = jnp.where(lane_full < 64, 128.0 * codes + turned, 128.0 * turned + codes)
    codes = jnp.where(lane_full // 64 == core, codes, 0.0)
    send_a[:, 0] = values.reshape(NU, NZ, 128)
    send_a[:, 1] = codes.reshape(NU, NZ, 128)

    pl.semaphore_wait(barrier, NU + NZ + NF - 3)

    def copy_a(k):
        peer = lax.rem(u + k, NU)
        return pltpu.make_async_remote_copy(
            send_a.at[peer], recv_a.at[u], a_send.at[k], a_recv.at[k],
            device_id={"shot": shot_of(z, peer)}, device_id_type=MESH,
        )

    for k in range(1, NU):
        copy_a(k).start()
    recv_a[u] = send_a[u]

    factor = math.sqrt(2.0)
    odd_m = 2 * lax.broadcasted_iota(jnp.int32, (64, HALF), 1) + 1

    @pl.loop(0, BINS // 64)
    def _(step):
        b = 2 * (lax.broadcasted_iota(jnp.int32, (64, HALF), 0) + step * 64) + 1
        cos, sin = sincos((4 + f) * odd_m * b * b)
        high, low = split(factor * cos)
        rows = pl.ds(pl.multiple_of(step * 64, 64), 64)
        table[rows, 0:HALF] = high
        table_low[rows, 0:HALF] = low
        high, low = split(factor * sin)
        table[rows, HALF:Q] = high
        table_low[rows, HALF:Q] = low

    for k in range(1, NU):
        copy_a(k).wait_recv()
    for i in range(NZ):
        send_b[i, 0:8] = recv_a[:, 0, i]
        send_b[i, 8:12] = recv_a[0:4, 1, i] + recv_a[4:8, 1, i]

    def copy_b(k):
        there = lax.rem(z + k, NZ)
        return pltpu.make_async_remote_copy(
            send_b.at[there], recv_b.at[z], b_send.at[k], b_recv.at[k],
            device_id={"shot": shot_of(there, u)}, device_id_type=MESH,
        )

    for k in (8, 7, 9, 6, 10, 5, 11, 4, 12, 3, 13, 2, 14, 1, 15):
        copy_b(k).start()
    recv_b[z] = send_b[z]

    odd_row = 2 * lax.broadcasted_iota(jnp.int32, (64, 128), 0) + 1

    @pl.loop(0, BINS // 128)
    def _(step):
        b = 2 * (lax.broadcasted_iota(jnp.int32, (64, 128), 1) + step * 128) + 1
        lanes = pl.ds(pl.multiple_of(step * 128, 128), 128)
        for part in range(2):
            rows = slice(part * 64, part * 64 + 64)
            cos, sin = sincos((4 + f) * (odd_row + part * 128) * b * b)
            high, low = split(factor * cos)
            table_t[rows, lanes] = high
            table_t_low[rows, lanes] = low
            rows = slice(HALF + part * 64, HALF + part * 64 + 64)
            high, low = split(factor * sin)
            table_t[rows, lanes] = high
            table_t_low[rows, lanes] = low

    b = 2 * lax.broadcasted_iota(jnp.int32, (1, BINS), 1) + 1
    shift_cos, shift_sin = sincos((4 + f) * (191 * b * b))
    flip = jnp.where(sub128 + lane_full == 127, 1.0, 0.0).astype(BF16)
    weight = weight_in[...]
    w_plus, w_minus = weight[:, HALF:], reverse_lanes(weight[:, :HALF], flip)

    lane4 = lax.broadcasted_iota(jnp.int32, (4, 128), 1)
    sub16 = lax.broadcasted_iota(jnp.int32, (16, 128), 0)
    row8 = lax.broadcasted_iota(jnp.int32, (8, 128), 0) & 3
    wanted = (((lane >> 4) & 3) - 2 * row8) & 3

    def turn(v):
        out = v
        for d in range(1, 4):
            moved = jnp.where(row8 + d < 4, pltpu.roll(v, 8 - d, 0), pltpu.roll(v, 4 - d, 0))
            out = jnp.where(wanted == d, moved, out)
        return out

    def bin_step(step, below, above, total):
        rows = pl.ds(pl.multiple_of(step * 8, 8), 8)
        re, im, code = [], [], []
        for at in (below, above):
            first, second = recv_b[at, 0:4], recv_b[at, 4:8]
            re.append(jnp.where(lane4 < 64, first, pltpu.roll(second, 64, 1)))
            im.append(jnp.where(lane4 < 64, pltpu.roll(first, 64, 1), second))
            code.append(recv_b[at, 8:12])
        re, im, code = (turn(jnp.concatenate(v, axis=0)) for v in (re, im, code))
        code = code.astype(jnp.int32)
        h, low = (code >> 7) - 1, code & 127
        row_h[rows, :] = h
        pieces = [p.astype(F32) for v in (re, im) for p in split(v)]
        for i in range(8):
            place = ((i % 4) * 2 + i // 4) * 128
            lanes = pl.ds(pl.multiple_of(step * GROUP + place, 128), 128)
            here = slice(place, place + 128)
            slot_low[:, lanes] = jnp.where(sub128 == low[i : i + 1], 1.0, 0.0).astype(BF16)
            mask = sub16 == h[i : i + 1]
            for j, piece in enumerate(pieces):
                slot_hot[16 * j : 16 * (j + 1), here] = jnp.where(mask, piece[i : i + 1], 0.0).astype(BF16)
            slot_hot[64:80, here] = jnp.where(mask, 1.0, 0.0).astype(BF16)
        out = []
        for quarter in range(4):
            lanes = pl.ds(pl.multiple_of(step * GROUP + quarter * 256, 128), 256)
            hot = slot_hot[:, quarter * 256 : quarter * 256 + 256]
            out.append(total[quarter] + mxu(hot, slot_low[:, lanes], NT))
        return tuple(out)

    def bin_pair(step, total):
        for k in (step + 1, NZ - 1 - step):
            copy_b(k).wait_recv()
        return bin_step(step, lax.rem(z + NZ - 1 - step, NZ), lax.rem(z + step + 1, NZ), total)

    binned = lax.fori_loop(0, 7, bin_pair, (jnp.zeros((80, 128), F32),) * 4)
    copy_b(8).wait_recv()
    binned = bin_step(7, z, lax.rem(z + 8, NZ), binned)

    def by_bin(quarters):
        return jnp.concatenate(
            [jnp.concatenate([v[4 * i : 4 * i + 4] for i in range(4)], axis=1) for v in quarters], axis=0
        )

    g_re = by_bin([v[0:16] + v[16:32] for v in binned])
    g_im = by_bin([v[32:48] + v[48:64] for v in binned])
    counts_ref[...] = by_bin([v[64:80] for v in binned])

    def product(v, high, low):
        n = v.shape[0]
        pieces = jnp.concatenate(split(v, 3), axis=0)
        main, rest = mxu(pieces, high), mxu(pieces[: 2 * n], low)
        return main[:n] + ((main[n : 2 * n] + rest[:n]) + (main[2 * n :] + rest[n:]))

    def forward(v):
        return product(v, table_t[...], table_t_low[...])

    def adjoint(g):
        return product(g, table[...], table_low[...])

    right_side = adjoint(
        jnp.concatenate([shift_cos * g_re - shift_sin * g_im, shift_cos * g_im + shift_sin * g_re], axis=0)
    )

    def inner(a, b):
        p = a * b
        return jnp.sum(p[:CMP] + p[CMP:], axis=1, keepdims=True)

    def both_parts(v):
        return jnp.concatenate([v, v], axis=0)

    def undamped(v):
        return adjoint(forward(v) * both_parts(counts_ref[...]))

    first_image = undamped(right_side)

    def solve(w_plus, w_minus):
        scale = 0.5 * MU_SCALE * BINS
        even, odd = scale * (w_plus + w_minus), scale * (w_plus - w_minus)

        def damp(v):
            s_re, s_im, t_re, t_im = v[:CMP, :HALF], v[CMP:, :HALF], v[:CMP, HALF:], v[CMP:, HALF:]
            return jnp.concatenate(
                [
                    jnp.concatenate([even * s_re - odd * t_im, even * t_re + odd * s_im], axis=1),
                    jnp.concatenate([even * s_im + odd * t_re, even * t_im - odd * s_re], axis=1),
                ],
                axis=0,
            )

        def image_of(direction):
            return undamped(direction) + damp(direction)

        def project(image, past, scales):
            out = image
            for old, scale in zip(past, scales):
                swapped = swap(old)
                along = both_parts(inner(old, image) * scale)
                across = both_parts(inner(swapped, image) * scale)
                out = out - (along * old + across * swapped)
            return out

        def swap(v):
            return jnp.concatenate([-v[CMP:], v[:CMP]], axis=0)

        def cg_step(state, past, scales, own):
            answer, residual, direction, norm_now = state
            image = first_image + damp(direction) if own and not past else image_of(direction)
            step = norm_now / inner(direction, image)
            coming = norm_now + step * (step * inner(image, image) - 2.0 * inner(residual, image))
            ratio = jnp.maximum(coming, 0.0) / norm_now
            kept = project(image, past, scales)
            if own:
                swapped = swap(residual)
                kept = kept - both_parts(inner(swapped, image) / norm_now) * swapped
            answer = answer + both_parts(step) * direction
            residual = residual - both_parts(step) * kept
            norm_next = inner(residual, residual)
            if not past:
                ratio = norm_next / norm_now
            direction = residual + both_parts(ratio) * direction
            return answer, residual, direction, norm_next

        state = (jnp.zeros_like(right_side), right_side, right_side, inner(right_side, right_side))
        past, scales = [], []
        for _ in range(KEPT):
            residual, norm = state[1], state[3]
            state = cg_step(state, tuple(past), scales, True)
            past.append(residual)
            scales.append(1.0 / norm)
        state = lax.fori_loop(
            KEPT, CG_STEPS - 1, lambda _, state: cg_step(state, past, scales, False), state
        )
        answer, _, direction, norm_now = state
        return answer + both_parts(norm_now / inner(direction, image_of(direction))) * direction

    def to_curvatures(v):
        root = math.sqrt(0.5)
        s_re, s_im, t_re, t_im = v[:CMP, :HALF], v[CMP:, :HALF], v[:CMP, HALF:], v[CMP:, HALF:]
        plus = root * (s_re - t_im), root * (s_im + t_re)
        minus = root * (s_re + t_im), root * (s_im - t_re)
        return plus, minus

    answer = solve(w_plus, w_minus)
    plus, minus = to_curvatures(answer)
    energy_own[:, :HALF] = plus[0] * plus[0] + plus[1] * plus[1]
    energy_own[:, HALF:] = minus[0] * minus[0] + minus[1] * minus[1]

    def copy_e(k):
        peer = lax.rem(f + k, NF)
        return pltpu.make_async_remote_copy(
            energy_own, energy_all.at[f], e_send.at[k], e_recv.at[k],
            device_id={"freq": peer}, device_id_type=MESH,
        )

    for k in (2, 1, 3):
        copy_e(k).start()
    energy_all[f] = energy_own[...]
    for k in (1, 3, 2):
        copy_e(k).wait_recv()
    energy = (energy_all[0] + energy_all[1]) + (energy_all[2] + energy_all[3])
    average = jnp.sum(energy, axis=1, keepdims=True) * (1.0 / Q)
    weight = (average + SMALL_EPS) / (energy + ENERGY_FLOOR * average + SMALL_EPS)
    answer = solve(weight[:, :HALF], weight[:, HALF:])
    plus, minus = to_curvatures(answer)

    root = math.sqrt(0.5)
    keep = lax.broadcasted_iota(jnp.int32, (CMP, HALF), 1) < 64
    low_re, low_im = jnp.where(keep, minus[0], 0.0), jnp.where(keep, minus[1], 0.0)
    masked = jnp.concatenate(
        [
            jnp.concatenate([root * (plus[0] + low_re), root * (plus[1] - low_im)], axis=1),
            jnp.concatenate([root * (plus[1] + low_im), root * (low_re - plus[0])], axis=1),
        ],
        axis=0,
    )
    field = forward(masked)
    p_re = shift_cos * field[:CMP] + shift_sin * field[CMP:]
    p_im = shift_cos * field[CMP:] - shift_sin * field[:CMP]
    predicted = jnp.concatenate(
        [
            p[4 * quarter : 4 * quarter + 4, 128 * i : 128 * i + 128]
            for quarter in range(4)
            for p in (p_re, p_im)
            for i in range(4)
        ],
        axis=0,
    )
    predicted = jnp.concatenate(split(predicted), axis=1)

    def copy_r(k):
        there = lax.rem(z + k, NZ)
        return pltpu.make_async_remote_copy(
            send_r.at[there], recv_r.at[z], r_send.at[k], r_recv.at[k],
            device_id={"shot": shot_of(there, u)}, device_id_type=MESH,
        )

    lane8 = lax.broadcasted_iota(jnp.int32, (8, 128), 1)

    def predict(step, below, above):
        rows = pl.ds(pl.multiple_of(step * 8, 8), 8)
        h = row_h[rows, :]
        got_re, got_im = [None] * 8, [None] * 8
        for quarter in range(4):
            low = slot_low[:, pl.ds(pl.multiple_of(step * GROUP + quarter * 256, 128), 256)]
            mine = predicted[32 * quarter : 32 * quarter + 32]
            found = mxu(mine, jnp.concatenate([low, low], axis=0))
            for part in range(2):
                i = part * 4 + quarter
                mask = sub16 == h[i : i + 1]
                here = slice(part * 128, part * 128 + 128)
                got_re[i] = jnp.sum(jnp.where(mask, found[:16, here], 0.0), axis=0, keepdims=True)
                got_im[i] = jnp.sum(jnp.where(mask, found[16:, here], 0.0), axis=0, keepdims=True)
        got_re, got_im = turn(jnp.concatenate(got_re, axis=0)), turn(jnp.concatenate(got_im, axis=0))
        first = jnp.where(lane8 < 64, got_re, pltpu.roll(got_im, 64, 1))
        second = jnp.where(lane8 < 64, pltpu.roll(got_re, 64, 1), got_im)
        for i, at in enumerate((below, above)):
            send_r[at, 0:4] = first[4 * i : 4 * i + 4]
            send_r[at, 4:8] = second[4 * i : 4 * i + 4]

    predict(7, z, lax.rem(z + 8, NZ))
    copy_r(8).start()
    recv_r[z] = send_r[z]

    @pl.loop(0, 7)
    def _(back):
        step = 6 - back
        predict(step, lax.rem(z + NZ - 1 - step, NZ), lax.rem(z + step + 1, NZ))
        copy_r(NZ - 1 - step).start()
        copy_r(step + 1).start()

    for part in range(2):
        radon_model[0, part, :, 0:HALF] = reverse_lanes(minus[part], flip)
        radon_model[0, part, :, HALF:Q] = plus[part]
    model_out = pltpu.make_async_copy(radon_model, radon_hbm, out_sems.at[0])
    model_out.start()

    for k in range(1, NZ):
        copy_r(k).wait_recv()

    def copy_t(k):
        peer = lax.rem(u + k, NU)
        return pltpu.make_async_remote_copy(
            recv_r.at[:, peer], recv_t.at[u], t_send.at[k], t_recv.at[k],
            device_id={"shot": shot_of(z, peer)}, device_id_type=MESH,
        )

    for k in range(1, NU):
        copy_t(k).start()
    recv_t[u] = recv_r[:, u]
    for k in range(1, NU):
        copy_t(k).wait_recv()

    def part_out(step):
        lanes = pl.ds(pl.multiple_of(step * GROUP, 128), GROUP)
        return pltpu.make_async_copy(
            primaries.at[:, :, lanes], primaries_hbm.at[:, :, lanes], out_sems.at[1 + step]
        )

    by_slot = jnp.concatenate(split(recv_t[...].reshape(128, 128).T), axis=1)

    @pl.loop(0, TRACES // GROUP)
    def _(step):
        rows = pl.ds(pl.multiple_of(step * 8, 8), 8)
        hot = dest_hot[:, pl.ds(pl.multiple_of(step * GROUP, 128), GROUP)]
        found = mxu(by_slot, jnp.concatenate([hot, hot], axis=0))
        within = row_s[rows, :]
        for i in range(8):
            mask = sub64 == within[i : i + 1]
            here = slice(i * 128, i * 128 + 128)
            lanes = pl.ds(pl.multiple_of(step * GROUP + i * 128, 128), 128)
            got = jnp.sum(jnp.where(mask, found[:64, here], 0.0), axis=0, keepdims=True)
            primaries[0, 0:1, lanes] = traces[0, 0:1, lanes] - got
            got = jnp.sum(jnp.where(mask, found[64:, here], 0.0), axis=0, keepdims=True)
            primaries[0, 1:2, lanes] = traces[0, 1:2, lanes] - got
        part_out(step).start()

    for k in range(1, NU):
        copy_a(k).wait_send()
        copy_t(k).wait_send()
    for k in range(1, NZ):
        copy_b(k).wait_send()
        copy_r(k).wait_send()
    for k in range(1, NF):
        copy_e(k).wait_send()
    model_out.wait()
    for step in range(TRACES // GROUP):
        part_out(step).wait()


def per_device(traces, trace_slot, trace_cmp, trace_bin, prior_weight):
    rows = TRACES // 128
    hbm = pl.BlockSpec(memory_space=pltpu.HBM)
    dma = pltpu.SemaphoreType.DMA
    return pl.pallas_call(
        kernel,
        out_shape=(
            jax.ShapeDtypeStruct((1, 2, TRACES), F32),
            jax.ShapeDtypeStruct((1, 2, CMP, Q), F32),
        ),
        in_specs=[hbm] * 5,
        out_specs=(hbm, hbm),
        scratch_shapes=[
            pltpu.VMEM((1, 2, TRACES), F32),
            pltpu.VMEM((rows, 128), jnp.int32),
            pltpu.VMEM((rows, 128), jnp.int32),
            pltpu.VMEM((rows, 128), jnp.int32),
            pltpu.VMEM((CMP, Q), F32),
            dma((5,)),
            pltpu.VMEM((1, 2, TRACES), F32),
            pltpu.VMEM((1, 2, CMP, Q), F32),
            dma((1 + TRACES // GROUP,)),
            pltpu.VMEM((128, TRACES), BF16),
            pltpu.VMEM((384, TRACES), BF16),
            pltpu.VMEM((128, 8192), BF16),
            pltpu.VMEM((80, GROUP), BF16),
            pltpu.VMEM((64, 128), jnp.int32),
            pltpu.VMEM((rows, 128), jnp.int32),
            pltpu.VMEM((BINS, Q), BF16),
            pltpu.VMEM((BINS, Q), BF16),
            pltpu.VMEM((Q, BINS), BF16),
            pltpu.VMEM((Q, BINS), BF16),
            pltpu.VMEM((CMP, BINS), F32),
            pltpu.VMEM((NU, 2, NZ, 128), F32),
            pltpu.VMEM((NU, 2, NZ, 128), F32),
            pltpu.VMEM((NZ, 12, 128), F32),
            pltpu.VMEM((NZ, 12, 128), F32),
            pltpu.VMEM((CMP, Q), F32),
            pltpu.VMEM((NF, CMP, Q), F32),
            pltpu.VMEM((NZ, NU, 128), F32),
            pltpu.VMEM((NZ, NU, 128), F32),
            pltpu.VMEM((NU, NZ, 128), F32),
            dma((NU,)), dma((NU,)), dma((NZ,)), dma((NZ,)),
            dma((NF,)), dma((NF,)), dma((NZ,)), dma((NZ,)), dma((NU,)), dma((NU,)),
        ],
        compiler_params=pltpu.CompilerParams(
            collective_id=0, has_side_effects=True, vmem_limit_bytes=56 * 1024 * 1024
        ),
        name="radon",
    )(
        traces,
        trace_slot.reshape(rows, 128),
        trace_cmp.reshape(rows, 128),
        trace_bin.reshape(rows, 128),
        prior_weight,
    )


def solution(mesh):
    return jax.shard_map(
        per_device,
        mesh=mesh,
        in_specs=(P("freq", None, "shot"), P("shot"), P("shot"), P("shot"), P("shot", None)),
        out_specs=(P("freq", None, "shot"), P("freq", None, "shot", None)),
        check_vma=False,
    )
```

```python
import math

import jax
import jax.numpy as jnp
from jax import lax
from jax.experimental import pallas as pl
from jax.experimental.pallas import tpu as pltpu
from jax.sharding import PartitionSpec as P

BINS = 512
Q = 256
HALF = 128
CG_STEPS = 8
KEPT = 3
MU_SCALE = 0.5
ENERGY_FLOOR = 0.5
SMALL_EPS = 1e-06

NZ = 16
NU = 8
NF = 4
CMP = 16
TRACES = 4096
GROUP = 1024
MESH = pl.DeviceIdType.MESH
F32 = jnp.float32
BF16 = jnp.bfloat16

NN = (((1,), (0,)), ((), ()))
NT = (((1,), (1,)), ((), ()))


def mxu(a, b, dims=NN):
    return lax.dot_general(a, b, dims, preferred_element_type=F32)


def split(v, pieces=2):
    out = [v.astype(BF16)]
    for _ in range(pieces - 1):
        v = v - out[-1].astype(F32)
        out.append(v.astype(BF16))
    return out


def reverse_lanes(v, flip):
    n = v.shape[0]
    out = mxu(jnp.concatenate(split(v, 3), axis=0), flip)
    return out[:n] + out[n : 2 * n] + out[2 * n :]


def sincos(k):
    quadrant = (k + (1 << 21)) >> 22
    rem = (k - (quadrant << 22)).astype(F32)
    t = rem * (2.0 * math.pi / (1 << 24))
    u = t * t
    s = t + t * u * (-1.0 / 6 + u * (1.0 / 120 + u * (-1.0 / 5040 + u * (1.0 / 362880))))
    c = 1.0 + u * (-0.5 + u * (1.0 / 24 + u * (-1.0 / 720 + u * (1.0 / 40320 + u * (-1.0 / 3628800)))))
    quadrant = quadrant & 3
    odd = (quadrant & 1) == 1
    cos = jnp.where(odd, s, c)
    sin = jnp.where(odd, c, s)
    cos = jnp.where((quadrant == 1) | (quadrant == 2), -cos, cos)
    sin = jnp.where(quadrant >= 2, -sin, sin)
    return cos, sin


def kernel(
    traces_hbm, slot_hbm, cmp_hbm, bin_hbm, weight_hbm, primaries_hbm, radon_hbm,
    traces, slot_in, cmp_in, bin_in, weight_in, in_sems, primaries, radon_model, out_sems,
    dest_hot, trace_hot, slot_low, slot_hot, row_h, row_s,
    table, table_low, table_t, table_t_low, counts_ref,
    send_a, recv_a, send_b, recv_b, energy_own, energy_all, send_r, recv_r, recv_t,
    a_send, a_recv, b_send, b_recv, e_send, e_recv, r_send, r_recv, t_send, t_recv,
):
    inputs = [
        pltpu.make_async_copy(source, target, in_sems.at[i])
        for i, (source, target) in enumerate(
            (
                (slot_hbm, slot_in),
                (traces_hbm, traces),
                (bin_hbm, bin_in),
                (cmp_hbm, cmp_in),
                (weight_hbm, weight_in),
            )
        )
    ]
    for copy in inputs:
        copy.start()

    shot = lax.axis_index("shot")
    f = lax.axis_index("freq")
    z = shot // NU
    x_core = lax.rem(shot, NU)
    core = lax.rem(x_core, 2)
    u = core * 4 + x_core // 2

    def shot_of(z_at, u_at):
        return z_at * NU + lax.rem(u_at, 4) * 2 + u_at // 4

    barrier = pltpu.get_barrier_semaphore()
    for k in range(1, NU):
        peer = shot_of(z, lax.rem(u + k, NU))
        pl.semaphore_signal(barrier, inc=1, device_id={"shot": peer}, device_id_type=MESH)
    for k in range(1, NZ):
        peer = shot_of(lax.rem(z + k, NZ), u)
        pl.semaphore_signal(barrier, inc=1, device_id={"shot": peer}, device_id_type=MESH)
    for k in range(1, NF):
        pl.semaphore_signal(barrier, inc=1, device_id={"freq": lax.rem(f + k, NF)}, device_id_type=MESH)

    lane = lax.broadcasted_iota(jnp.int32, (8, 128), 1)
    sub64 = lax.broadcasted_iota(jnp.int32, (64, 128), 0)
    sub128 = lax.broadcasted_iota(jnp.int32, (128, 128), 0)

    for copy in inputs:
        copy.wait()

    @pl.loop(0, TRACES // GROUP, unroll=True)
    def _(step):
        rows = pl.ds(pl.multiple_of(step * 8, 8), 8)
        slot, bins = slot_in[rows, :], bin_in[rows, :]
        dest = (((slot >> 6) & 1) * 4 + ((slot >> 7) & 3)) * NZ + (slot >> 9)
        within = (slot + 16 * lax.rem(u, 4)) & 63
        row_s[rows, :] = within
        high = (bins >> 7) * 4 + cmp_in[rows, :] + 1
        low = bins & 127
        high, low = high.astype(F32), low.astype(F32)
        for i in range(8):
            lanes = pl.ds(pl.multiple_of(step * GROUP + i * 128, 128), 128)
            re_h, re_l = split(traces[0, 0:1, lanes])
            im_h, im_l = split(traces[0, 1:2, lanes])
            dest_hot[:, lanes] = jnp.where(sub128 == dest[i : i + 1], 1.0, 0.0).astype(BF16)
            mask = sub64 == within[i : i + 1]
            for j, piece in enumerate((re_h, im_h, re_l, im_l, high[i : i + 1], low[i : i + 1])):
                trace_hot[64 * j : 64 * (j + 1), lanes] = jnp.where(mask, piece.astype(F32), 0.0).astype(BF16)

    placed = mxu(dest_hot[...], trace_hot[...], NT)
    values = placed[:, 0:128] + placed[:, 128:256]
    codes = placed[:, 256:384]
    turned = pltpu.roll(codes, 64, 1)
    lane_full = lax.broadcasted_iota(jnp.int32, (128, 128), 1)
    codes = jnp.where(lane_full < 64, 128.0 * codes + turned, 128.0 * turned + codes)
    codes = jnp.where(lane_full // 64 == core, codes, 0.0)
    send_a[:, 0] = values.reshape(NU, NZ, 128)
    send_a[:, 1] = codes.reshape(NU, NZ, 128)

    pl.semaphore_wait(barrier, NU + NZ + NF - 3)

    def copy_a(k):
        peer = lax.rem(u + k, NU)
        return pltpu.make_async_remote_copy(
            send_a.at[peer], recv_a.at[u], a_send.at[k], a_recv.at[k],
            device_id={"shot": shot_of(z, peer)}, device_id_type=MESH,
        )

    for k in range(1, NU):
        copy_a(k).start()
    recv_a[u] = send_a[u]

    factor = math.sqrt(2.0)
    odd_m = 2 * lax.broadcasted_iota(jnp.int32, (64, HALF), 1) + 1

    @pl.loop(0, BINS // 64)
    def _(step):
        b = 2 * (lax.broadcasted_iota(jnp.int32, (64, HALF), 0) + step * 64) + 1
        cos, sin = sincos((4 + f) * odd_m * b * b)
        high, low = split(factor * cos)
        rows = pl.ds(pl.multiple_of(step * 64, 64), 64)
        table[rows, 0:HALF] = high
        table_low[rows, 0:HALF] = low
        high, low = split(factor * sin)
        table[rows, HALF:Q] = high
        table_low[rows, HALF:Q] = low

    for k in range(1, NU):
        copy_a(k).wait_recv()
    for i in range(NZ):
        send_b[i, 0:8] = recv_a[:, 0, i]
        send_b[i, 8:12] = recv_a[0:4, 1, i] + recv_a[4:8, 1, i]

    def copy_b(k):
        there = lax.rem(z + k, NZ)
        return pltpu.make_async_remote_copy(
            send_b.at[there], recv_b.at[z], b_send.at[k], b_recv.at[k],
            device_id={"shot": shot_of(there, u)}, device_id_type=MESH,
        )

    for k in (8, 7, 9, 6, 10, 5, 11, 4, 12, 3, 13, 2, 14, 1, 15):
        copy_b(k).start()
    recv_b[z] = send_b[z]

    odd_row = 2 * lax.broadcasted_iota(jnp.int32, (64, 128), 0) + 1

    @pl.loop(0, BINS // 128)
    def _(step):
        b = 2 * (lax.broadcasted_iota(jnp.int32, (64, 128), 1) + step * 128) + 1
        lanes = pl.ds(pl.multiple_of(step * 128, 128), 128)
        for part in range(2):
            rows = slice(part * 64, part * 64 + 64)
            cos, sin = sincos((4 + f) * (odd_row + part * 128) * b * b)
            high, low = split(factor * cos)
            table_t[rows, lanes] = high
            table_t_low[rows, lanes] = low
            rows = slice(HALF + part * 64, HALF + part * 64 + 64)
            high, low = split(factor * sin)
            table_t[rows, lanes] = high
            table_t_low[rows, lanes] = low

    b = 2 * lax.broadcasted_iota(jnp.int32, (1, BINS), 1) + 1
    shift_cos, shift_sin = sincos((4 + f) * (191 * b * b))
    flip = jnp.where(sub128 + lane_full == 127, 1.0, 0.0).astype(BF16)
    weight = weight_in[...]
    w_plus, w_minus = weight[:, HALF:], reverse_lanes(weight[:, :HALF], flip)

    lane4 = lax.broadcasted_iota(jnp.int32, (4, 128), 1)
    sub16 = lax.broadcasted_iota(jnp.int32, (16, 128), 0)
    row8 = lax.broadcasted_iota(jnp.int32, (8, 128), 0) & 3
    wanted = (((lane >> 4) & 3) - 2 * row8) & 3

    def turn(v):
        out = v
        for d in range(1, 4):
            moved = jnp.where(row8 + d < 4, pltpu.roll(v, 8 - d, 0), pltpu.roll(v, 4 - d, 0))
            out = jnp.where(wanted == d, moved, out)
        return out

    def bin_step(step, below, above, total):
        rows = pl.ds(pl.multiple_of(step * 8, 8), 8)
        re, im, code = [], [], []
        for at in (below, above):
            first, second = recv_b[at, 0:4], recv_b[at, 4:8]
            re.append(jnp.where(lane4 < 64, first, pltpu.roll(second, 64, 1)))
            im.append(jnp.where(lane4 < 64, pltpu.roll(first, 64, 1), second))
            code.append(recv_b[at, 8:12])
        re, im, code = (turn(jnp.concatenate(v, axis=0)) for v in (re, im, code))
        code = code.astype(jnp.int32)
        h, low = (code >> 7) - 1, code & 127
        row_h[rows, :] = h
        pieces = [p.astype(F32) for v in (re, im) for p in split(v)]
        for i in range(8):
            place = ((i % 4) * 2 + i // 4) * 128
            lanes = pl.ds(pl.multiple_of(step * GROUP + place, 128), 128)
            here = slice(place, place + 128)
            slot_low[:, lanes] = jnp.where(sub128 == low[i : i + 1], 1.0, 0.0).astype(BF16)
            mask = sub16 == h[i : i + 1]
            for j, piece in enumerate(pieces):
                slot_hot[16 * j : 16 * (j + 1), here] = jnp.where(mask, piece[i : i + 1], 0.0).astype(BF16)
            slot_hot[64:80, here] = jnp.where(mask, 1.0, 0.0).astype(BF16)
        out = []
        for quarter in range(4):
            lanes = pl.ds(pl.multiple_of(step * GROUP + quarter * 256, 128), 256)
            hot = slot_hot[:, quarter * 256 : quarter * 256 + 256]
            out.append(total[quarter] + mxu(hot, slot_low[:, lanes], NT))
        return tuple(out)

    def bin_pair(step, total):
        for k in (step + 1, NZ - 1 - step):
            copy_b(k).wait_recv()
        return bin_step(step, lax.rem(z + NZ - 1 - step, NZ), lax.rem(z + step + 1, NZ), total)

    binned = lax.fori_loop(0, 7, bin_pair, (jnp.zeros((80, 128), F32),) * 4)
    copy_b(8).wait_recv()
    binned = bin_step(7, z, lax.rem(z + 8, NZ), binned)

    def by_bin(quarters):
        return jnp.concatenate(
            [jnp.concatenate([v[4 * i : 4 * i + 4] for i in range(4)], axis=1) for v in quarters], axis=0
        )

    g_re = by_bin([v[0:16] + v[16:32] for v in binned])
    g_im = by_bin([v[32:48] + v[48:64] for v in binned])
    counts_ref[...] = by_bin([v[64:80] for v in binned])

    def product(v, high, low):
        n = v.shape[0]
        pieces = jnp.concatenate(split(v, 3), axis=0)
        main, rest = mxu(pieces, high), mxu(pieces[: 2 * n], low)
        return main[:n] + ((main[n : 2 * n] + rest[:n]) + (main[2 * n :] + rest[n:]))

    def forward(v):
        return product(v, table_t[...], table_t_low[...])

    def adjoint(g):
        return product(g, table[...], table_low[...])

    right_side = adjoint(
        jnp.concatenate([shift_cos * g_re - shift_sin * g_im, shift_cos * g_im + shift_sin * g_re], axis=0)
    )

    def inner(a, b):
        p = a * b
        return jnp.sum(p[:CMP] + p[CMP:], axis=1, keepdims=True)

    def both_parts(v):
        return jnp.concatenate([v, v], axis=0)

    def undamped(v):
        return adjoint(forward(v) * both_parts(counts_ref[...]))

    first_image = undamped(right_side)

    def solve(w_plus, w_minus):
        scale = 0.5 * MU_SCALE * BINS
        even, odd = scale * (w_plus + w_minus), scale * (w_plus - w_minus)

        def damp(v):
            s_re, s_im, t_re, t_im = v[:CMP, :HALF], v[CMP:, :HALF], v[:CMP, HALF:], v[CMP:, HALF:]
            return jnp.concatenate(
                [
                    jnp.concatenate([even * s_re - odd * t_im, even * t_re + odd * s_im], axis=1),
                    jnp.concatenate([even * s_im + odd * t_re, even * t_im - odd * s_re], axis=1),
                ],
                axis=0,
            )

        def image_of(direction):
            return undamped(direction) + damp(direction)

        def project(image, past, scales):
            out = image
            for old, scale in zip(past, scales):
                swapped = swap(old)
                along = both_parts(inner(old, image) * scale)
                across = both_parts(inner(swapped, image) * scale)
                out = out - (along * old + across * swapped)
            return out

        def swap(v):
            return jnp.concatenate([-v[CMP:], v[:CMP]], axis=0)

        def cg_step(state, past, scales, own):
            answer, residual, direction, norm_now = state
            image = first_image + damp(direction) if own and not past else image_of(direction)
            step = norm_now / inner(direction, image)
            coming = norm_now + step * (step * inner(image, image) - 2.0 * inner(residual, image))
            ratio = jnp.maximum(coming, 0.0) / norm_now
            kept = project(image, past, scales)
            if own:
                swapped = swap(residual)
                kept = kept - both_parts(inner(swapped, image) / norm_now) * swapped
            answer = answer + both_parts(step) * direction
            residual = residual - both_parts(step) * kept
            norm_next = inner(residual, residual)
            if not past:
                ratio = norm_next / norm_now
            direction = residual + both_parts(ratio) * direction
            return answer, residual, direction, norm_next

        state = (jnp.zeros_like(right_side), right_side, right_side, inner(right_side, right_side))
        past, scales = [], []
        for _ in range(KEPT):
            residual, norm = state[1], state[3]
            state = cg_step(state, tuple(past), scales, True)
            past.append(residual)
            scales.append(1.0 / norm)
        for _ in range(KEPT, CG_STEPS - 1):
            state = cg_step(state, past, scales, False)
        answer, _, direction, norm_now = state
        return answer + both_parts(norm_now / inner(direction, image_of(direction))) * direction

    def to_curvatures(v):
        root = math.sqrt(0.5)
        s_re, s_im, t_re, t_im = v[:CMP, :HALF], v[CMP:, :HALF], v[:CMP, HALF:], v[CMP:, HALF:]
        plus = root * (s_re - t_im), root * (s_im + t_re)
        minus = root * (s_re + t_im), root * (s_im - t_re)
        return plus, minus

    answer = solve(w_plus, w_minus)
    plus, minus = to_curvatures(answer)
    energy_own[:, :HALF] = plus[0] * plus[0] + plus[1] * plus[1]
    energy_own[:, HALF:] = minus[0] * minus[0] + minus[1] * minus[1]

    def copy_e(k):
        peer = lax.rem(f + k, NF)
        return pltpu.make_async_remote_copy(
            energy_own, energy_all.at[f], e_send.at[k], e_recv.at[k],
            device_id={"freq": peer}, device_id_type=MESH,
        )

    for k in (2, 1, 3):
        copy_e(k).start()
    energy_all[f] = energy_own[...]
    for k in (1, 3, 2):
        copy_e(k).wait_recv()
    energy = (energy_all[0] + energy_all[1]) + (energy_all[2] + energy_all[3])
    average = jnp.sum(energy, axis=1, keepdims=True) * (1.0 / Q)
    weight = (average + SMALL_EPS) / (energy + ENERGY_FLOOR * average + SMALL_EPS)
    answer = solve(weight[:, :HALF], weight[:, HALF:])
    plus, minus = to_curvatures(answer)

    root = math.sqrt(0.5)
    keep = lax.broadcasted_iota(jnp.int32, (CMP, HALF), 1) < 64
    low_re, low_im = jnp.where(keep, minus[0], 0.0), jnp.where(keep, minus[1], 0.0)
    masked = jnp.concatenate(
        [
            jnp.concatenate([root * (plus[0] + low_re), root * (plus[1] - low_im)], axis=1),
            jnp.concatenate([root * (plus[1] + low_im), root * (low_re - plus[0])], axis=1),
        ],
        axis=0,
    )
    field = forward(masked)
    p_re = shift_cos * field[:CMP] + shift_sin * field[CMP:]
    p_im = shift_cos * field[CMP:] - shift_sin * field[:CMP]
    predicted = jnp.concatenate(
        [
            p[4 * quarter : 4 * quarter + 4, 128 * i : 128 * i + 128]
            for quarter in range(4)
            for p in (p_re, p_im)
            for i in range(4)
        ],
        axis=0,
    )
    predicted = jnp.concatenate(split(predicted), axis=1)

    def copy_r(k):
        there = lax.rem(z + k, NZ)
        return pltpu.make_async_remote_copy(
            send_r.at[there], recv_r.at[z], r_send.at[k], r_recv.at[k],
            device_id={"shot": shot_of(there, u)}, device_id_type=MESH,
        )

    lane8 = lax.broadcasted_iota(jnp.int32, (8, 128), 1)

    def predict(step, below, above):
        rows = pl.ds(pl.multiple_of(step * 8, 8), 8)
        h = row_h[rows, :]
        got_re, got_im = [None] * 8, [None] * 8
        for quarter in range(4):
            low = slot_low[:, pl.ds(pl.multiple_of(step * GROUP + quarter * 256, 128), 256)]
            mine = predicted[32 * quarter : 32 * quarter + 32]
            found = mxu(mine, jnp.concatenate([low, low], axis=0))
            for part in range(2):
                i = part * 4 + quarter
                mask = sub16 == h[i : i + 1]
                here = slice(part * 128, part * 128 + 128)
                got_re[i] = jnp.sum(jnp.where(mask, found[:16, here], 0.0), axis=0, keepdims=True)
                got_im[i] = jnp.sum(jnp.where(mask, found[16:, here], 0.0), axis=0, keepdims=True)
        got_re, got_im = turn(jnp.concatenate(got_re, axis=0)), turn(jnp.concatenate(got_im, axis=0))
        first = jnp.where(lane8 < 64, got_re, pltpu.roll(got_im, 64, 1))
        second = jnp.where(lane8 < 64, pltpu.roll(got_re, 64, 1), got_im)
        for i, at in enumerate((below, above)):
            send_r[at, 0:4] = first[4 * i : 4 * i + 4]
            send_r[at, 4:8] = second[4 * i : 4 * i + 4]

    predict(7, z, lax.rem(z + 8, NZ))
    copy_r(8).start()
    recv_r[z] = send_r[z]

    @pl.loop(0, 7, unroll=True)
    def _(back):
        step = 6 - back
        predict(step, lax.rem(z + NZ - 1 - step, NZ), lax.rem(z + step + 1, NZ))
        copy_r(NZ - 1 - step).start()
        copy_r(step + 1).start()

    for part in range(2):
        radon_model[0, part, :, 0:HALF] = reverse_lanes(minus[part], flip)
        radon_model[0, part, :, HALF:Q] = plus[part]
    model_out = pltpu.make_async_copy(radon_model, radon_hbm, out_sems.at[0])
    model_out.start()

    for k in range(1, NZ):
        copy_r(k).wait_recv()

    def copy_t(k):
        peer = lax.rem(u + k, NU)
        return pltpu.make_async_remote_copy(
            recv_r.at[:, peer], recv_t.at[u], t_send.at[k], t_recv.at[k],
            device_id={"shot": shot_of(z, peer)}, device_id_type=MESH,
        )

    for k in range(1, NU):
        copy_t(k).start()
    recv_t[u] = recv_r[:, u]
    for k in range(1, NU):
        copy_t(k).wait_recv()

    def part_out(step):
        lanes = pl.ds(pl.multiple_of(step * GROUP, 128), GROUP)
        return pltpu.make_async_copy(
            primaries.at[:, :, lanes], primaries_hbm.at[:, :, lanes], out_sems.at[1 + step]
        )

    by_slot = jnp.concatenate(split(recv_t[...].reshape(128, 128).T), axis=1)

    @pl.loop(0, TRACES // GROUP, unroll=True)
    def _(step):
        rows = pl.ds(pl.multiple_of(step * 8, 8), 8)
        hot = dest_hot[:, pl.ds(pl.multiple_of(step * GROUP, 128), GROUP)]
        found = mxu(by_slot, jnp.concatenate([hot, hot], axis=0))
        within = row_s[rows, :]
        for i in range(8):
            mask = sub64 == within[i : i + 1]
            here = slice(i * 128, i * 128 + 128)
            lanes = pl.ds(pl.multiple_of(step * GROUP + i * 128, 128), 128)
            got = jnp.sum(jnp.where(mask, found[:64, here], 0.0), axis=0, keepdims=True)
            primaries[0, 0:1, lanes] = traces[0, 0:1, lanes] - got
            got = jnp.sum(jnp.where(mask, found[64:, here], 0.0), axis=0, keepdims=True)
            primaries[0, 1:2, lanes] = traces[0, 1:2, lanes] - got
        part_out(step).start()

    for k in range(1, NU):
        copy_a(k).wait_send()
        copy_t(k).wait_send()
    for k in range(1, NZ):
        copy_b(k).wait_send()
        copy_r(k).wait_send()
    for k in range(1, NF):
        copy_e(k).wait_send()
    model_out.wait()
    for step in range(TRACES // GROUP):
        part_out(step).wait()


def per_device(traces, trace_slot, trace_cmp, trace_bin, prior_weight):
    rows = TRACES // 128
    hbm = pl.BlockSpec(memory_space=pltpu.HBM)
    dma = pltpu.SemaphoreType.DMA
    return pl.pallas_call(
        kernel,
        out_shape=(
            jax.ShapeDtypeStruct((1, 2, TRACES), F32),
            jax.ShapeDtypeStruct((1, 2, CMP, Q), F32),
        ),
        in_specs=[hbm] * 5,
        out_specs=(hbm, hbm),
        scratch_shapes=[
            pltpu.VMEM((1, 2, TRACES), F32),
            pltpu.VMEM((rows, 128), jnp.int32),
            pltpu.VMEM((rows, 128), jnp.int32),
            pltpu.VMEM((rows, 128), jnp.int32),
            pltpu.VMEM((CMP, Q), F32),
            dma((5,)),
            pltpu.VMEM((1, 2, TRACES), F32),
            pltpu.VMEM((1, 2, CMP, Q), F32),
            dma((1 + TRACES // GROUP,)),
            pltpu.VMEM((128, TRACES), BF16),
            pltpu.VMEM((384, TRACES), BF16),
            pltpu.VMEM((128, 8192), BF16),
            pltpu.VMEM((80, GROUP), BF16),
            pltpu.VMEM((64, 128), jnp.int32),
            pltpu.VMEM((rows, 128), jnp.int32),
            pltpu.VMEM((BINS, Q), BF16),
            pltpu.VMEM((BINS, Q), BF16),
            pltpu.VMEM((Q, BINS), BF16),
            pltpu.VMEM((Q, BINS), BF16),
            pltpu.VMEM((CMP, BINS), F32),
            pltpu.VMEM((NU, 2, NZ, 128), F32),
            pltpu.VMEM((NU, 2, NZ, 128), F32),
            pltpu.VMEM((NZ, 12, 128), F32),
            pltpu.VMEM((NZ, 12, 128), F32),
            pltpu.VMEM((CMP, Q), F32),
            pltpu.VMEM((NF, CMP, Q), F32),
            pltpu.VMEM((NZ, NU, 128), F32),
            pltpu.VMEM((NZ, NU, 128), F32),
            pltpu.VMEM((NU, NZ, 128), F32),
            dma((NU,)), dma((NU,)), dma((NZ,)), dma((NZ,)),
            dma((NF,)), dma((NF,)), dma((NZ,)), dma((NZ,)), dma((NU,)), dma((NU,)),
        ],
        compiler_params=pltpu.CompilerParams(
            collective_id=0, has_side_effects=True, vmem_limit_bytes=56 * 1024 * 1024
        ),
        name="radon",
    )(
        traces,
        trace_slot.reshape(rows, 128),
        trace_cmp.reshape(rows, 128),
        trace_bin.reshape(rows, 128),
        prior_weight,
    )


def solution(mesh):
    return jax.shard_map(
        per_device,
        mesh=mesh,
        in_specs=(P("freq", None, "shot"), P("shot"), P("shot"), P("shot"), P("shot", None)),
        out_specs=(P("freq", None, "shot"), P("freq", None, "shot", None)),
        check_vma=False,
    )
```

```python
import math

import jax
import jax.numpy as jnp
from jax import lax
from jax.experimental import pallas as pl
from jax.experimental.pallas import tpu as pltpu
from jax.sharding import PartitionSpec as P

BINS = 512
Q = 256
HALF = 128
CG_STEPS = 8
KEPT = 3
MU_SCALE = 0.5
ENERGY_FLOOR = 0.5
SMALL_EPS = 1e-06

NZ = 16
NU = 8
NF = 4
CMP = 16
TRACES = 4096
GROUP = 1024
MESH = pl.DeviceIdType.MESH
F32 = jnp.float32
BF16 = jnp.bfloat16

NN = (((1,), (0,)), ((), ()))
NT = (((1,), (1,)), ((), ()))


def mxu(a, b, dims=NN):
    return lax.dot_general(a, b, dims, preferred_element_type=F32)


def split(v, pieces=2):
    out = [v.astype(BF16)]
    for _ in range(pieces - 1):
        v = v - out[-1].astype(F32)
        out.append(v.astype(BF16))
    return out


def reverse_lanes(v, flip):
    n = v.shape[0]
    out = mxu(jnp.concatenate(split(v, 3), axis=0), flip)
    return out[:n] + out[n : 2 * n] + out[2 * n :]


def sincos(k):
    quadrant = (k + (1 << 21)) >> 22
    rem = (k - (quadrant << 22)).astype(F32)
    t = rem * (2.0 * math.pi / (1 << 24))
    u = t * t
    s = t + t * u * (-1.0 / 6 + u * (1.0 / 120 + u * (-1.0 / 5040 + u * (1.0 / 362880))))
    c = 1.0 + u * (-0.5 + u * (1.0 / 24 + u * (-1.0 / 720 + u * (1.0 / 40320 + u * (-1.0 / 3628800)))))
    quadrant = quadrant & 3
    odd = (quadrant & 1) == 1
    cos = jnp.where(odd, s, c)
    sin = jnp.where(odd, c, s)
    cos = jnp.where((quadrant == 1) | (quadrant == 2), -cos, cos)
    sin = jnp.where(quadrant >= 2, -sin, sin)
    return cos, sin


def kernel(
    traces_hbm, slot_hbm, cmp_hbm, bin_hbm, weight_hbm, primaries_hbm, radon_hbm,
    traces, slot_in, cmp_in, bin_in, weight_in, in_sems, primaries, radon_model, out_sems,
    dest_hot, trace_hot, slot_low, slot_hot, row_h, row_s,
    table, table_low, table_t, table_t_low, counts_ref,
    send_a, recv_a, send_b, recv_b, energy_own, energy_all, send_r, recv_r, recv_t,
    a_send, a_recv, b_send, b_recv, e_send, e_recv, r_send, r_recv, t_send, t_recv,
):
    inputs = [
        pltpu.make_async_copy(source, target, in_sems.at[i])
        for i, (source, target) in enumerate(
            (
                (slot_hbm, slot_in),
                (traces_hbm, traces),
                (bin_hbm, bin_in),
                (cmp_hbm, cmp_in),
                (weight_hbm, weight_in),
            )
        )
    ]
    for copy in inputs:
        copy.start()

    shot = lax.axis_index("shot")
    f = lax.axis_index("freq")
    z = shot // NU
    x_core = lax.rem(shot, NU)
    core = lax.rem(x_core, 2)
    u = core * 4 + x_core // 2

    def shot_of(z_at, u_at):
        return z_at * NU + lax.rem(u_at, 4) * 2 + u_at // 4

    barrier = pltpu.get_barrier_semaphore()
    for k in range(1, NU):
        peer = shot_of(z, lax.rem(u + k, NU))
        pl.semaphore_signal(barrier, inc=1, device_id={"shot": peer}, device_id_type=MESH)
    for k in range(1, NZ):
        peer = shot_of(lax.rem(z + k, NZ), u)
        pl.semaphore_signal(barrier, inc=1, device_id={"shot": peer}, device_id_type=MESH)
    for k in range(1, NF):
        pl.semaphore_signal(barrier, inc=1, device_id={"freq": lax.rem(f + k, NF)}, device_id_type=MESH)

    lane = lax.broadcasted_iota(jnp.int32, (8, 128), 1)
    sub64 = lax.broadcasted_iota(jnp.int32, (64, 128), 0)
    sub128 = lax.broadcasted_iota(jnp.int32, (128, 128), 0)

    for copy in inputs:
        copy.wait()

    @pl.loop(0, TRACES // GROUP, unroll=True)
    def _(step):
        rows = pl.ds(pl.multiple_of(step * 8, 8), 8)
        slot, bins = slot_in[rows, :], bin_in[rows, :]
        dest = (((slot >> 6) & 1) * 4 + ((slot >> 7) & 3)) * NZ + (slot >> 9)
        within = (slot + 16 * lax.rem(u, 4)) & 63
        row_s[rows, :] = within
        high = (bins >> 7) * 4 + cmp_in[rows, :] + 1
        low = bins & 127
        high, low = high.astype(F32), low.astype(F32)
        for i in range(8):
            lanes = pl.ds(pl.multiple_of(step * GROUP + i * 128, 128), 128)
            re_h, re_l = split(traces[0, 0:1, lanes])
            im_h, im_l = split(traces[0, 1:2, lanes])
            dest_hot[:, lanes] = jnp.where(sub128 == dest[i : i + 1], 1.0, 0.0).astype(BF16)
            mask = sub64 == within[i : i + 1]
            for j, piece in enumerate((re_h, im_h, re_l, im_l, high[i : i + 1], low[i : i + 1])):
                trace_hot[64 * j : 64 * (j + 1), lanes] = jnp.where(mask, piece.astype(F32), 0.0).astype(BF16)

    placed = mxu(dest_hot[...], trace_hot[...], NT)
    values = placed[:, 0:128] + placed[:, 128:256]
    codes = placed[:, 256:384]
    turned = pltpu.roll(codes, 64, 1)
    lane_full = lax.broadcasted_iota(jnp.int32, (128, 128), 1)
    codes = jnp.where(lane_full < 64, 128.0 * codes + turned, 128.0 * turned + codes)
    codes = jnp.where(lane_full // 64 == core, codes, 0.0)
    send_a[:, 0] = values.reshape(NU, NZ, 128)
    send_a[:, 1] = codes.reshape(NU, NZ, 128)

    pl.semaphore_wait(barrier, NU + NZ + NF - 3)

    def copy_a(k):
        peer = lax.rem(u + k, NU)
        return pltpu.make_async_remote_copy(
            send_a.at[peer], recv_a.at[u], a_send.at[k], a_recv.at[k],
            device_id={"shot": shot_of(z, peer)}, device_id_type=MESH,
        )

    for k in range(1, NU):
        copy_a(k).start()
    recv_a[u] = send_a[u]

    factor = math.sqrt(2.0)
    odd_m = 2 * lax.broadcasted_iota(jnp.int32, (64, HALF), 1) + 1

    @pl.loop(0, BINS // 64)
    def _(step):
        b = 2 * (lax.broadcasted_iota(jnp.int32, (64, HALF), 0) + step * 64) + 1
        cos, sin = sincos((4 + f) * odd_m * b * b)
        high, low = split(factor * cos)
        rows = pl.ds(pl.multiple_of(step * 64, 64), 64)
        table[rows, 0:HALF] = high
        table_low[rows, 0:HALF] = low
        high, low = split(factor * sin)
        table[rows, HALF:Q] = high
        table_low[rows, HALF:Q] = low

    for k in range(1, NU):
        copy_a(k).wait_recv()
    for i in range(NZ):
        send_b[i, 0:8] = recv_a[:, 0, i]
        send_b[i, 8:12] = recv_a[0:4, 1, i] + recv_a[4:8, 1, i]

    def copy_b(k):
        there = lax.rem(z + k, NZ)
        return pltpu.make_async_remote_copy(
            send_b.at[there], recv_b.at[z], b_send.at[k], b_recv.at[k],
            device_id={"shot": shot_of(there, u)}, device_id_type=MESH,
        )

    for k in (8, 7, 9, 6, 10, 5, 11, 4, 12, 3, 13, 2, 14, 1, 15):
        copy_b(k).start()
    recv_b[z] = send_b[z]

    odd_row = 2 * lax.broadcasted_iota(jnp.int32, (64, 128), 0) + 1

    @pl.loop(0, BINS // 128)
    def _(step):
        b = 2 * (lax.broadcasted_iota(jnp.int32, (64, 128), 1) + step * 128) + 1
        lanes = pl.ds(pl.multiple_of(step * 128, 128), 128)
        for part in range(2):
            rows = slice(part * 64, part * 64 + 64)
            cos, sin = sincos((4 + f) * (odd_row + part * 128) * b * b)
            high, low = split(factor * cos)
            table_t[rows, lanes] = high
            table_t_low[rows, lanes] = low
            rows = slice(HALF + part * 64, HALF + part * 64 + 64)
            high, low = split(factor * sin)
            table_t[rows, lanes] = high
            table_t_low[rows, lanes] = low

    b = 2 * lax.broadcasted_iota(jnp.int32, (1, BINS), 1) + 1
    shift_cos, shift_sin = sincos((4 + f) * (191 * b * b))
    flip = jnp.where(sub128 + lane_full == 127, 1.0, 0.0).astype(BF16)
    weight = weight_in[...]
    w_plus, w_minus = weight[:, HALF:], reverse_lanes(weight[:, :HALF], flip)

    lane4 = lax.broadcasted_iota(jnp.int32, (4, 128), 1)
    sub16 = lax.broadcasted_iota(jnp.int32, (16, 128), 0)
    row8 = lax.broadcasted_iota(jnp.int32, (8, 128), 0) & 3
    wanted = (((lane >> 4) & 3) - 2 * row8) & 3

    def turn(v):
        out = v
        for d in range(1, 4):
            moved = jnp.where(row8 + d < 4, pltpu.roll(v, 8 - d, 0), pltpu.roll(v, 4 - d, 0))
            out = jnp.where(wanted == d, moved, out)
        return out

    def bin_step(step, below, above, total):
        rows = pl.ds(pl.multiple_of(step * 8, 8), 8)
        re, im, code = [], [], []
        for at in (below, above):
            first, second = recv_b[at, 0:4], recv_b[at, 4:8]
            re.append(jnp.where(lane4 < 64, first, pltpu.roll(second, 64, 1)))
            im.append(jnp.where(lane4 < 64, pltpu.roll(first, 64, 1), second))
            code.append(recv_b[at, 8:12])
        re, im, code = (turn(jnp.concatenate(v, axis=0)) for v in (re, im, code))
        code = code.astype(jnp.int32)
        h, low = (code >> 7) - 1, code & 127
        row_h[rows, :] = h
        pieces = [p.astype(F32) for v in (re, im) for p in split(v)]
        for i in range(8):
            place = ((i % 4) * 2 + i // 4) * 128
            lanes = pl.ds(pl.multiple_of(step * GROUP + place, 128), 128)
            here = slice(place, place + 128)
            slot_low[:, lanes] = jnp.where(sub128 == low[i : i + 1], 1.0, 0.0).astype(BF16)
            mask = sub16 == h[i : i + 1]
            for j, piece in enumerate(pieces):
                slot_hot[16 * j : 16 * (j + 1), here] = jnp.where(mask, piece[i : i + 1], 0.0).astype(BF16)
            slot_hot[64:80, here] = jnp.where(mask, 1.0, 0.0).astype(BF16)
        out = []
        for quarter in range(4):
            lanes = pl.ds(pl.multiple_of(step * GROUP + quarter * 256, 128), 256)
            hot = slot_hot[:, quarter * 256 : quarter * 256 + 256]
            out.append(total[quarter] + mxu(hot, slot_low[:, lanes], NT))
        return tuple(out)

    def bin_pair(step, total):
        for k in (step + 1, NZ - 1 - step):
            copy_b(k).wait_recv()
        return bin_step(step, lax.rem(z + NZ - 1 - step, NZ), lax.rem(z + step + 1, NZ), total)

    binned = lax.fori_loop(0, 7, bin_pair, (jnp.zeros((80, 128), F32),) * 4, unroll=True)
    copy_b(8).wait_recv()
    binned = bin_step(7, z, lax.rem(z + 8, NZ), binned)

    def by_bin(quarters):
        return jnp.concatenate(
            [jnp.concatenate([v[4 * i : 4 * i + 4] for i in range(4)], axis=1) for v in quarters], axis=0
        )

    g_re = by_bin([v[0:16] + v[16:32] for v in binned])
    g_im = by_bin([v[32:48] + v[48:64] for v in binned])
    counts_ref[...] = by_bin([v[64:80] for v in binned])

    def product(v, high, low):
        n = v.shape[0]
        pieces = jnp.concatenate(split(v, 3), axis=0)
        main, rest = mxu(pieces, high), mxu(pieces[: 2 * n], low)
        return main[:n] + ((main[n : 2 * n] + rest[:n]) + (main[2 * n :] + rest[n:]))

    def forward(v):
        return product(v, table_t[...], table_t_low[...])

    def adjoint(g):
        return product(g, table[...], table_low[...])

    right_side = adjoint(
        jnp.concatenate([shift_cos * g_re - shift_sin * g_im, shift_cos * g_im + shift_sin * g_re], axis=0)
    )

    def inner(a, b):
        p = a * b
        return jnp.sum(p[:CMP] + p[CMP:], axis=1, keepdims=True)

    def both_parts(v):
        return jnp.concatenate([v, v], axis=0)

    def undamped(v):
        return adjoint(forward(v) * both_parts(counts_ref[...]))

    first_image = undamped(right_side)

    def solve(w_plus, w_minus):
        scale = 0.5 * MU_SCALE * BINS
        even, odd = scale * (w_plus + w_minus), scale * (w_plus - w_minus)

        def damp(v):
            s_re, s_im, t_re, t_im = v[:CMP, :HALF], v[CMP:, :HALF], v[:CMP, HALF:], v[CMP:, HALF:]
            return jnp.concatenate(
                [
                    jnp.concatenate([even * s_re - odd * t_im, even * t_re + odd * s_im], axis=1),
                    jnp.concatenate([even * s_im + odd * t_re, even * t_im - odd * s_re], axis=1),
                ],
                axis=0,
            )

        def image_of(direction):
            return undamped(direction) + damp(direction)

        def project(image, past, scales):
            out = image
            for old, scale in zip(past, scales):
                swapped = swap(old)
                along = both_parts(inner(old, image) * scale)
                across = both_parts(inner(swapped, image) * scale)
                out = out - (along * old + across * swapped)
            return out

        def swap(v):
            return jnp.concatenate([-v[CMP:], v[:CMP]], axis=0)

        def cg_step(state, past, scales, own):
            answer, residual, direction, norm_now = state
            image = first_image + damp(direction) if own and not past else image_of(direction)
            step = norm_now / inner(direction, image)
            coming = norm_now + step * (step * inner(image, image) - 2.0 * inner(residual, image))
            ratio = jnp.maximum(coming, 0.0) / norm_now
            kept = project(image, past, scales)
            if own:
                swapped = swap(residual)
                kept = kept - both_parts(inner(swapped, image) / norm_now) * swapped
            answer = answer + both_parts(step) * direction
            residual = residual - both_parts(step) * kept
            norm_next = inner(residual, residual)
            if not past:
                ratio = norm_next / norm_now
            direction = residual + both_parts(ratio) * direction
            return answer, residual, direction, norm_next

        state = (jnp.zeros_like(right_side), right_side, right_side, inner(right_side, right_side))
        past, scales = [], []
        for _ in range(KEPT):
            residual, norm = state[1], state[3]
            state = cg_step(state, tuple(past), scales, True)
            past.append(residual)
            scales.append(1.0 / norm)
        for _ in range(KEPT, CG_STEPS - 1):
            state = cg_step(state, past, scales, False)
        answer, _, direction, norm_now = state
        return answer + both_parts(norm_now / inner(direction, image_of(direction))) * direction

    def to_curvatures(v):
        root = math.sqrt(0.5)
        s_re, s_im, t_re, t_im = v[:CMP, :HALF], v[CMP:, :HALF], v[:CMP, HALF:], v[CMP:, HALF:]
        plus = root * (s_re - t_im), root * (s_im + t_re)
        minus = root * (s_re + t_im), root * (s_im - t_re)
        return plus, minus

    answer = solve(w_plus, w_minus)
    plus, minus = to_curvatures(answer)
    energy_own[:, :HALF] = plus[0] * plus[0] + plus[1] * plus[1]
    energy_own[:, HALF:] = minus[0] * minus[0] + minus[1] * minus[1]

    def copy_e(k):
        peer = lax.rem(f + k, NF)
        return pltpu.make_async_remote_copy(
            energy_own, energy_all.at[f], e_send.at[k], e_recv.at[k],
            device_id={"freq": peer}, device_id_type=MESH,
        )

    for k in (2, 1, 3):
        copy_e(k).start()
    energy_all[f] = energy_own[...]
    for k in (1, 3, 2):
        copy_e(k).wait_recv()
    energy = (energy_all[0] + energy_all[1]) + (energy_all[2] + energy_all[3])
    average = jnp.sum(energy, axis=1, keepdims=True) * (1.0 / Q)
    weight = (average + SMALL_EPS) / (energy + ENERGY_FLOOR * average + SMALL_EPS)
    answer = solve(weight[:, :HALF], weight[:, HALF:])
    plus, minus = to_curvatures(answer)

    root = math.sqrt(0.5)
    keep = lax.broadcasted_iota(jnp.int32, (CMP, HALF), 1) < 64
    low_re, low_im = jnp.where(keep, minus[0], 0.0), jnp.where(keep, minus[1], 0.0)
    masked = jnp.concatenate(
        [
            jnp.concatenate([root * (plus[0] + low_re), root * (plus[1] - low_im)], axis=1),
            jnp.concatenate([root * (plus[1] + low_im), root * (low_re - plus[0])], axis=1),
        ],
        axis=0,
    )
    field = forward(masked)
    p_re = shift_cos * field[:CMP] + shift_sin * field[CMP:]
    p_im = shift_cos * field[CMP:] - shift_sin * field[:CMP]
    predicted = jnp.concatenate(
        [
            p[4 * quarter : 4 * quarter + 4, 128 * i : 128 * i + 128]
            for quarter in range(4)
            for p in (p_re, p_im)
            for i in range(4)
        ],
        axis=0,
    )
    predicted = jnp.concatenate(split(predicted), axis=1)

    def copy_r(k):
        there = lax.rem(z + k, NZ)
        return pltpu.make_async_remote_copy(
            send_r.at[there], recv_r.at[z], r_send.at[k], r_recv.at[k],
            device_id={"shot": shot_of(there, u)}, device_id_type=MESH,
        )

    lane8 = lax.broadcasted_iota(jnp.int32, (8, 128), 1)

    def predict(step, below, above):
        rows = pl.ds(pl.multiple_of(step * 8, 8), 8)
        h = row_h[rows, :]
        got_re, got_im = [None] * 8, [None] * 8
        for quarter in range(4):
            low = slot_low[:, pl.ds(pl.multiple_of(step * GROUP + quarter * 256, 128), 256)]
            mine = predicted[32 * quarter : 32 * quarter + 32]
            found = mxu(mine, jnp.concatenate([low, low], axis=0))
            for part in range(2):
                i = part * 4 + quarter
                mask = sub16 == h[i : i + 1]
                here = slice(part * 128, part * 128 + 128)
                got_re[i] = jnp.sum(jnp.where(mask, found[:16, here], 0.0), axis=0, keepdims=True)
                got_im[i] = jnp.sum(jnp.where(mask, found[16:, here], 0.0), axis=0, keepdims=True)
        got_re, got_im = turn(jnp.concatenate(got_re, axis=0)), turn(jnp.concatenate(got_im, axis=0))
        first = jnp.where(lane8 < 64, got_re, pltpu.roll(got_im, 64, 1))
        second = jnp.where(lane8 < 64, pltpu.roll(got_re, 64, 1), got_im)
        for i, at in enumerate((below, above)):
            send_r[at, 0:4] = first[4 * i : 4 * i + 4]
            send_r[at, 4:8] = second[4 * i : 4 * i + 4]

    predict(7, z, lax.rem(z + 8, NZ))
    copy_r(8).start()
    recv_r[z] = send_r[z]

    @pl.loop(0, 7, unroll=True)
    def _(back):
        step = 6 - back
        predict(step, lax.rem(z + NZ - 1 - step, NZ), lax.rem(z + step + 1, NZ))
        copy_r(NZ - 1 - step).start()
        copy_r(step + 1).start()

    for part in range(2):
        radon_model[0, part, :, 0:HALF] = reverse_lanes(minus[part], flip)
        radon_model[0, part, :, HALF:Q] = plus[part]
    model_out = pltpu.make_async_copy(radon_model, radon_hbm, out_sems.at[0])
    model_out.start()

    for k in range(1, NU):
        copy_a(k).wait_send()
    for k in range(1, NZ):
        copy_b(k).wait_send()
    for k in range(1, NF):
        copy_e(k).wait_send()
    for k in range(1, NZ):
        copy_r(k).wait_recv()

    def copy_t(k):
        peer = lax.rem(u + k, NU)
        return pltpu.make_async_remote_copy(
            recv_r.at[:, peer], recv_t.at[u], t_send.at[k], t_recv.at[k],
            device_id={"shot": shot_of(z, peer)}, device_id_type=MESH,
        )

    for k in range(1, NU):
        copy_t(k).start()
    recv_t[u] = recv_r[:, u]
    for k in range(1, NZ):
        copy_r(k).wait_send()
    for k in range(1, NU):
        copy_t(k).wait_recv()

    def part_out(step):
        lanes = pl.ds(pl.multiple_of(step * GROUP, 128), GROUP)
        return pltpu.make_async_copy(
            primaries.at[:, :, lanes], primaries_hbm.at[:, :, lanes], out_sems.at[1 + step]
        )

    by_slot = jnp.concatenate(split(recv_t[...].reshape(128, 128).T), axis=1)

    @pl.loop(0, TRACES // GROUP, unroll=True)
    def _(step):
        rows = pl.ds(pl.multiple_of(step * 8, 8), 8)
        hot = dest_hot[:, pl.ds(pl.multiple_of(step * GROUP, 128), GROUP)]
        found = mxu(by_slot, jnp.concatenate([hot, hot], axis=0))
        within = row_s[rows, :]
        for i in range(8):
            mask = sub64 == within[i : i + 1]
            here = slice(i * 128, i * 128 + 128)
            lanes = pl.ds(pl.multiple_of(step * GROUP + i * 128, 128), 128)
            got = jnp.sum(jnp.where(mask, found[:64, here], 0.0), axis=0, keepdims=True)
            primaries[0, 0:1, lanes] = traces[0, 0:1, lanes] - got
            got = jnp.sum(jnp.where(mask, found[64:, here], 0.0), axis=0, keepdims=True)
            primaries[0, 1:2, lanes] = traces[0, 1:2, lanes] - got
        part_out(step).start()

    for k in range(1, NU):
        copy_t(k).wait_send()
    model_out.wait()
    for step in range(TRACES // GROUP):
        part_out(step).wait()


def per_device(traces, trace_slot, trace_cmp, trace_bin, prior_weight):
    rows = TRACES // 128
    hbm = pl.BlockSpec(memory_space=pltpu.HBM)
    dma = pltpu.SemaphoreType.DMA
    return pl.pallas_call(
        kernel,
        out_shape=(
            jax.ShapeDtypeStruct((1, 2, TRACES), F32),
            jax.ShapeDtypeStruct((1, 2, CMP, Q), F32),
        ),
        in_specs=[hbm] * 5,
        out_specs=(hbm, hbm),
        scratch_shapes=[
            pltpu.VMEM((1, 2, TRACES), F32),
            pltpu.VMEM((rows, 128), jnp.int32),
            pltpu.VMEM((rows, 128), jnp.int32),
            pltpu.VMEM((rows, 128), jnp.int32),
            pltpu.VMEM((CMP, Q), F32),
            dma((5,)),
            pltpu.VMEM((1, 2, TRACES), F32),
            pltpu.VMEM((1, 2, CMP, Q), F32),
            dma((1 + TRACES // GROUP,)),
            pltpu.VMEM((128, TRACES), BF16),
            pltpu.VMEM((384, TRACES), BF16),
            pltpu.VMEM((128, 8192), BF16),
            pltpu.VMEM((80, GROUP), BF16),
            pltpu.VMEM((64, 128), jnp.int32),
            pltpu.VMEM((rows, 128), jnp.int32),
            pltpu.VMEM((BINS, Q), BF16),
            pltpu.VMEM((BINS, Q), BF16),
            pltpu.VMEM((Q, BINS), BF16),
            pltpu.VMEM((Q, BINS), BF16),
            pltpu.VMEM((CMP, BINS), F32),
            pltpu.VMEM((NU, 2, NZ, 128), F32),
            pltpu.VMEM((NU, 2, NZ, 128), F32),
            pltpu.VMEM((NZ, 12, 128), F32),
            pltpu.VMEM((NZ, 12, 128), F32),
            pltpu.VMEM((CMP, Q), F32),
            pltpu.VMEM((NF, CMP, Q), F32),
            pltpu.VMEM((NZ, NU, 128), F32),
            pltpu.VMEM((NZ, NU, 128), F32),
            pltpu.VMEM((NU, NZ, 128), F32),
            dma((NU,)), dma((NU,)), dma((NZ,)), dma((NZ,)),
            dma((NF,)), dma((NF,)), dma((NZ,)), dma((NZ,)), dma((NU,)), dma((NU,)),
        ],
        compiler_params=pltpu.CompilerParams(
            collective_id=0, has_side_effects=True, vmem_limit_bytes=56 * 1024 * 1024
        ),
        name="radon",
    )(
        traces,
        trace_slot.reshape(rows, 128),
        trace_cmp.reshape(rows, 128),
        trace_bin.reshape(rows, 128),
        prior_weight,
    )


def solution(mesh):
    return jax.shard_map(
        per_device,
        mesh=mesh,
        in_specs=(P("freq", None, "shot"), P("shot"), P("shot"), P("shot"), P("shot", None)),
        out_specs=(P("freq", None, "shot"), P("freq", None, "shot", None)),
        check_vma=False,
    )
```
